512 devices in a mesh: seq: 32 (over y, x, core), head: 16 (over z).
Axes of the slice: x: 4, y: 4, z: 16, core: 2. Of those that a mesh axis runs over, the one named last changes fastest.
Arguments:
- inputs: bfloat16 [1024, 16384], P('head', 'seq'), may hold values from -6 to 6
- grad_out: bfloat16 [1024, 16384], P('head', 'seq'), may hold values from -6 to 6
- keys_b: bfloat16 [16384, 128], P('seq'), may hold values from -0.25 to 0.25
- queries_c: bfloat16 [16384, 128], P('seq'), may hold values from -0.5 to 0.5
- level_gates: float32 [144, 16384], P('head', 'seq'), may hold values from 0.25 to 1.5
- log_decay: float32 [16, 16384], P('head', 'seq'), may hold values from -1 to 0
- doc_starts: int32 [256], P('seq'), may hold values from 0 to 1, as said below
Outputs:
- grad_inputs: bfloat16 [1024, 16384], P('head', 'seq')
- grad_keys: bfloat16 [16384, 128], P(('seq', 'head'))
- grad_queries: bfloat16 [16384, 128], P(('seq', 'head'))
- grad_gates: float32 [144, 16384], P('head', 'seq')
- grad_decay: float32 [16, 16384], P('head', 'seq')
The draws below stay inside these ranges and needn't reach their ends.
Inputs may be any that keep to these rules, and one draw needn't show every extreme that they name: `doc_starts`: ones lie only in the first 8 spans and in the last 8 spans, and each of these two ranges holds at least one.
All inputs are finite; a program needn't handle non-finite values.
Results may differ from the reference program's by a relative error of at most 0.0032.
Values sent between devices are 32-bit elements; how exact they have to be, the bound alone decides.
No kernel may reach another device: no remote copies, remote signals or barrier semaphores. Data moves between devices by JAX's collectives and lax.ppermute only.
A program may use at most 64 MiB of HBM per device.

```python
import jax
import jax.numpy as jnp
from jax import lax

P_SIZE = 64
N = 128
LIVE_ATTENDERS = 16
SPAN = 64
CH_LOG = 3
CH_DEV = 8
TOK_DEV = 512
STREAM_ELEMENTS = 16384
NCHUNK = 256
LEVELS = 9
N_SEQ = 32


def draw_log_decay(key, part):
    key = jax.random.fold_in(key, 7)
    stochastic_seedlets = jax.random.split(key, 7)
    slow_share = 0.5
    slow_heads = jax.random.uniform(stochastic_seedlets[0], (LIVE_ATTENDERS, 1)) < slow_share
    fast_rate = jax.random.uniform(stochastic_seedlets[1], (LIVE_ATTENDERS, 1), minval=0.02, maxval=0.034)
    slow_rate = jax.random.uniform(stochastic_seedlets[2], (LIVE_ATTENDERS, 1), minval=0.2, maxval=0.8) / STREAM_ELEMENTS
    forgetting_rate = jnp.where(slow_heads, slow_rate, fast_rate)
    shard_count = STREAM_ELEMENTS // TOK_DEV
    partition_factor = jax.random.uniform(stochastic_seedlets[3], (LIVE_ATTENDERS, shard_count, 1), minval=0.7, maxval=1.4)
    partition_factor = jnp.broadcast_to(partition_factor, (LIVE_ATTENDERS, shard_count, TOK_DEV)).reshape(LIVE_ATTENDERS, STREAM_ELEMENTS)
    irregular_spread = jax.random.uniform(stochastic_seedlets[4], (LIVE_ATTENDERS, STREAM_ELEMENTS), minval=0.5, maxval=1.5)
    cluster_offset = jax.random.randint(stochastic_seedlets[5], (LIVE_ATTENDERS, 3, 1), 0, STREAM_ELEMENTS)
    cluster_extent = jax.random.uniform(stochastic_seedlets[6], (LIVE_ATTENDERS, 3, 1), minval=-0.69, maxval=-0.22)
    element_indices = jnp.arange(STREAM_ELEMENTS)[None, None, :]
    cluster_tally = jnp.sum(jnp.where(element_indices == cluster_offset, cluster_extent, 0.0), axis=1)
    return (-forgetting_rate * partition_factor * irregular_spread + cluster_tally).astype(jnp.float32)


def draw_doc_starts(key, part):
    key = jax.random.fold_in(key, 11)
    start_keys = jax.random.split(key, 3)
    span_index = jnp.arange(NCHUNK, dtype=jnp.int32)
    in_first = span_index < CH_DEV
    in_last = span_index >= NCHUNK - CH_DEV
    first_pick = jax.random.randint(start_keys[0], (), 0, CH_DEV)
    last_pick = jax.random.randint(start_keys[1], (), NCHUNK - CH_DEV, NCHUNK)
    extra_marks = jax.random.randint(start_keys[2], (NCHUNK,), 0, 4) == 0
    starts = (span_index == first_pick) | (span_index == last_pick) | extra_marks & (in_first | in_last)
    return starts.astype(jnp.int32)


def steps_of(stream_key, shape, pieces, smallest, top_value):
    def one(axis_at, parts):
        heights = jax.random.uniform(jax.random.fold_in(jax.random.fold_in(stream_key, 6), axis_at), (parts,), jnp.float32, smallest / len(pieces), top_value / len(pieces))
        return jnp.repeat(jnp.exp(heights), shape[axis_at] // parts).reshape((-1,) + (1,) * (len(shape) - axis_at - 1))

    gain = one(*pieces[0])
    for cut in pieces[1:]:
        gain = gain * one(*cut)
    return gain


def centred(rng, shape, deviation, limit, shards=(), kind=jnp.bfloat16):
    values = deviation * jax.random.normal(rng, shape, jnp.float32)
    if shards:
        values = values * steps_of(rng, shape, shards, -0.22, 0.18)
    return jnp.clip(values, -limit, limit).astype(kind)


def setup_inputs(seed: int = 0) -> dict:
    key_of = jax.random.split(jax.random.key(seed), 8)
    return {
        "inputs": centred(key_of[0], (LIVE_ATTENDERS * P_SIZE, STREAM_ELEMENTS), 1.0, 6.0, ((0, 16), (1, 32))),
        "grad_out": centred(key_of[1], (LIVE_ATTENDERS * P_SIZE, STREAM_ELEMENTS), 1.0, 6.0, ((0, 16), (1, 32))),
        "keys_b": centred(key_of[2], (STREAM_ELEMENTS, N), TOK_DEV ** -0.5, 0.25, ((0, 32),)),
        "queries_c": centred(key_of[3], (STREAM_ELEMENTS, N), N ** -0.5, 0.5, ((0, 32),)),
        "level_gates": jnp.clip(0.25 + 1.25 * jax.random.uniform(key_of[4], (LIVE_ATTENDERS * LEVELS, STREAM_ELEMENTS), jnp.float32) ** steps_of(key_of[4], (LIVE_ATTENDERS * LEVELS, STREAM_ELEMENTS), ((0, 16), (1, 32)), -0.2, 0.2), 0.25, 1.5),
        "log_decay": draw_log_decay(jax.random.fold_in(key_of[7], 71), 0),
        "doc_starts": draw_doc_starts(jax.random.fold_in(key_of[7], 71), 0),
    }


PRECISE = lax.Precision.HIGHEST


def product(left, right, pattern):
    return jnp.einsum(pattern, left.astype(jnp.float32), right.astype(jnp.float32), precision=PRECISE)


def quadratic_terms(head_inputs, head_grads, head_gates, running, counts, span_ids, key_rows, query_rows, local_depth):
    tokens = running.shape[0]
    block_rows = min(512, tokens)
    grad_vals = jnp.zeros(head_inputs.shape, jnp.float32)
    key_grad = jnp.zeros(key_rows.shape, jnp.float32)
    run_grad = jnp.zeros((tokens,), jnp.float32)
    query_parts = []
    gate_parts = []
    key_pos = jnp.arange(tokens, dtype=jnp.int32)
    for first_row in range(0, tokens, block_rows):
        last_row = first_row + block_rows
        query_pos = key_pos[first_row:last_row]
        spread = running[first_row:last_row, None] - running[None, :]
        valid_pair = (key_pos[None, :] <= query_pos[:, None]) & (counts[first_row:last_row, None] == counts[None, :])
        decay_mat = jnp.where(valid_pair, jnp.exp(jnp.minimum(spread, 0.0)), 0.0)
        xor_bits = jnp.bitwise_xor(span_ids[first_row:last_row, None], span_ids[None, :])
        level_map = sum((xor_bits >= (1 << digit_pos)).astype(jnp.int32) for digit_pos in range(local_depth))
        gate_block = head_gates[:, first_row:last_row]
        chosen = jnp.zeros(decay_mat.shape, jnp.float32)
        for level_num in range(local_depth + 1):
            chosen = chosen + jnp.where(level_map == level_num, gate_block[level_num][:, None], 0.0)
        weight_mat = chosen * decay_mat
        scores = product(query_rows[first_row:last_row], key_rows, "tn,sn->ts")
        kernel = scores * weight_mat
        kernel_low = kernel.astype(jnp.bfloat16)
        kernel_grad = product(head_grads[:, first_row:last_row], head_inputs, "pt,ps->ts")
        grad_vals = grad_vals + product(head_grads[:, first_row:last_row], kernel_low, "pt,ts->ps")
        score_grad = (kernel_grad * weight_mat).astype(jnp.bfloat16)
        query_parts.append(product(score_grad, key_rows, "ts,sn->tn"))
        key_grad = key_grad + product(score_grad, query_rows[first_row:last_row], "ts,tn->sn")
        flow_mat = kernel_grad * kernel
        run_grad = run_grad - jnp.sum(flow_mat, axis=0)
        run_grad = run_grad.at[first_row:last_row].add(jnp.sum(flow_mat, axis=1))
        gate_terms = kernel_grad * scores * decay_mat
        gate_parts.append(jnp.stack([jnp.sum(jnp.where(level_map == level_num, gate_terms, 0.0), axis=1) for level_num in range(local_depth + 1)]))
    return grad_vals, key_grad, jnp.concatenate(query_parts, 0), run_grad, jnp.concatenate(gate_parts, 1)


def shard_states(head_inputs, head_grads, head_gates, running, counts, key_rows, query_rows, local_depth):
    last_run = running[-1]
    entry_gain = jnp.where(counts == 0, jnp.exp(running), 0.0)
    leave_gain = jnp.where(counts == counts[-1], jnp.exp(last_run - running), 0.0)
    shard_gain = jnp.where(counts[-1] == 0, jnp.exp(last_run), 0.0)
    keys_scaled = key_rows.astype(jnp.float32) * leave_gain[:, None]
    end_state = jnp.einsum("tn,pt->np", keys_scaled, head_inputs.astype(jnp.float32), precision=PRECISE)
    cross_gates = head_gates[local_depth + 1:] * entry_gain[None, :]
    scaled_grads = cross_gates[:, None, :] * head_grads.astype(jnp.float32)[None]
    state_grad = jnp.einsum("mpt,tn->mnp", scaled_grads, query_rows.astype(jnp.float32), precision=PRECISE)
    return end_state, state_grad, shard_gain, entry_gain, leave_gain


def chain_inputs(end_state, state_grad, shard_gain, upper_bits, not_first, not_last):
    gain_fwd = shard_gain[..., None] * not_first.astype(jnp.float32)
    push_fwd = jnp.where(upper_bits[..., None, None] == 0, end_state[..., None, :, :], 0.0)
    gain_back = shard_gain[..., None] * not_last.astype(jnp.float32)
    push_back = jnp.where(upper_bits[..., None, None] == 1, state_grad, 0.0)
    return (gain_fwd, push_fwd), (gain_back, push_back)


def chain_results(prefix_states, suffix_states, upper_bits, not_first, not_last):
    carried = jnp.where(upper_bits[..., None, None] == 1, prefix_states, 0.0)
    returned = jnp.sum(jnp.where(upper_bits[..., None, None] == 0, suffix_states, 0.0), axis=-3)
    gain_grad = jnp.sum(jnp.where(not_first[..., None, None], prefix_states, 0.0) * jnp.where(not_last[..., None, None], suffix_states, 0.0), axis=(-3, -2, -1))
    return carried, returned, gain_grad


def cross_terms(head_inputs, head_grads, head_gates, key_rows, query_rows, local_depth, carried, returned, entry_gain, leave_gain):
    grads_wide = head_grads.astype(jnp.float32)
    inputs_wide = head_inputs.astype(jnp.float32)
    keys_wide = key_rows.astype(jnp.float32)
    mixed_state = jnp.einsum("mnp,pt->mnt", carried, grads_wide, precision=PRECISE)
    cross_value = jnp.sum(mixed_state * query_rows.astype(jnp.float32).T[None], axis=1)
    cross_gates = head_gates[local_depth + 1:]
    grad_gate = cross_value * entry_gain[None, :]
    query_grad = jnp.einsum("mt,mnt->tn", cross_gates * entry_gain[None, :], mixed_state, precision=PRECISE)
    run_grad = entry_gain * jnp.sum(cross_gates * cross_value, axis=0)
    pulled = jnp.einsum("np,tn->pt", returned, keys_wide, precision=PRECISE) * leave_gain[None, :]
    pushed = jnp.einsum("np,pt->tn", returned, inputs_wide, precision=PRECISE)
    key_grad = pushed * leave_gain[:, None]
    pushed_flow = jnp.sum(pushed * keys_wide, axis=1) * leave_gain
    run_grad = run_grad - pushed_flow
    last_grad = jnp.sum(pushed_flow)
    return pulled, key_grad, query_grad, grad_gate, run_grad, last_grad


def assemble(quad_parts, cross_parts, gain_grad, shard_gain):
    quad_vals, quad_keys, quad_queries, quad_run, quad_gates = quad_parts
    cross_vals, cross_keys, cross_queries, cross_gate, cross_run, cross_last = cross_parts
    run_grad = quad_run + cross_run
    run_grad = run_grad.at[-1].add(cross_last + gain_grad * shard_gain)
    decay_grad = jnp.flip(jnp.cumsum(jnp.flip(run_grad)))
    return quad_vals + cross_vals, quad_keys + cross_keys, quad_queries + cross_queries, jnp.concatenate([quad_gates, cross_gate], 0), decay_grad


def reference(inputs, grad_out, keys_b, queries_c, level_gates, log_decay, doc_starts):
    shard_count = N_SEQ
    local_depth = CH_LOG
    head_count = log_decay.shape[0]
    channels = inputs.shape[0] // head_count
    level_count = level_gates.shape[0] // head_count
    seq_depth = level_count - local_depth - 1
    shard_tokens = log_decay.shape[1] // shard_count
    state_size = keys_b.shape[1]
    counts_all = jnp.repeat(jnp.cumsum(doc_starts.reshape(shard_count, -1), axis=1, dtype=jnp.int32), SPAN, axis=1)
    span_ids = jnp.arange(shard_tokens, dtype=jnp.int32) // SPAN
    keys_seg = keys_b.reshape(shard_count, shard_tokens, state_size)
    queries_seg = queries_c.reshape(shard_count, shard_tokens, state_size)
    inputs_seg = inputs.reshape(head_count, channels, shard_count, shard_tokens).transpose(0, 2, 1, 3)
    grads_seg = grad_out.reshape(head_count, channels, shard_count, shard_tokens).transpose(0, 2, 1, 3)
    gates_seg = level_gates.reshape(head_count, level_count, shard_count, shard_tokens).transpose(0, 2, 1, 3)
    decay_seg = log_decay.reshape(head_count, shard_count, shard_tokens)
    shard_ids = jnp.arange(shard_count, dtype=jnp.int32)
    level_ids = jnp.arange(seq_depth, dtype=jnp.int32)
    upper_bits = jnp.right_shift(shard_ids[:, None], level_ids[None, :]) & 1
    block_size = jnp.left_shift(jnp.int32(2), level_ids)
    not_first = (shard_ids[:, None] % block_size[None, :]) != 0
    not_last = ((shard_ids[:, None] + 1) % block_size[None, :]) != 0

    def chain_step(carry_state, item_pair):
        gain_item, push_item = item_pair
        return gain_item[:, None, None] * carry_state + push_item, carry_state

    def one_head(totals, head_in):
        head_inputs, head_grads, head_gates, head_decay = head_in

        def local_part(segment):
            seg_inputs, seg_grads, seg_gates, seg_decay, seg_counts, seg_keys, seg_queries = segment
            running = jnp.cumsum(seg_decay)
            quad_parts = quadratic_terms(seg_inputs, seg_grads, seg_gates, running, seg_counts, span_ids, seg_keys, seg_queries, local_depth)
            state_parts = shard_states(seg_inputs, seg_grads, seg_gates, running, seg_counts, seg_keys, seg_queries, local_depth)
            return quad_parts, state_parts

        quad_parts, state_parts = lax.map(local_part, (head_inputs, head_grads, head_gates, head_decay, counts_all, keys_seg, queries_seg))
        end_state, state_grad, shard_gain, entry_gain, leave_gain = state_parts
        forward_in, backward_in = chain_inputs(end_state, state_grad, shard_gain, upper_bits, not_first, not_last)
        zero_state = jnp.zeros((seq_depth, state_size, channels), jnp.float32)
        _, prefix_states = lax.scan(chain_step, zero_state, forward_in)
        _, suffix_states = lax.scan(chain_step, zero_state, backward_in, reverse=True)
        carried, returned, gain_grad = chain_results(prefix_states, suffix_states, upper_bits, not_first, not_last)

        def cross_part(segment):
            seg_inputs, seg_grads, seg_gates, seg_keys, seg_queries, seg_carried, seg_returned, seg_entry, seg_leave, seg_quad, seg_gain_grad, seg_gain = segment
            cross_parts = cross_terms(seg_inputs, seg_grads, seg_gates, seg_keys, seg_queries, local_depth, seg_carried, seg_returned, seg_entry, seg_leave)
            return assemble(seg_quad, cross_parts, seg_gain_grad, seg_gain)

        grad_vals, key_grad, query_grad, gate_grad, decay_grad = lax.map(cross_part, (head_inputs, head_grads, head_gates, keys_seg, queries_seg, carried, returned, entry_gain, leave_gain, quad_parts, gain_grad, shard_gain))
        return (totals[0] + key_grad, totals[1] + query_grad), (grad_vals, gate_grad, decay_grad)

    zero_rows = jnp.zeros((shard_count, shard_tokens, state_size), jnp.float32)
    totals, per_head = lax.scan(one_head, (zero_rows, zero_rows), (inputs_seg, grads_seg, gates_seg, decay_seg))
    grad_vals, gate_grad, decay_grad = per_head
    grad_inputs = grad_vals.transpose(0, 2, 1, 3).reshape(head_count * channels, shard_count * shard_tokens).astype(jnp.bfloat16)
    grad_keys = totals[0].reshape(shard_count * shard_tokens, state_size).astype(jnp.bfloat16)
    grad_queries = totals[1].reshape(shard_count * shard_tokens, state_size).astype(jnp.bfloat16)
    grad_gates = gate_grad.transpose(0, 2, 1, 3).reshape(head_count * level_count, shard_count * shard_tokens)
    grad_decay = decay_grad.reshape(head_count, shard_count * shard_tokens)
    return grad_inputs, grad_keys, grad_queries, grad_gates, grad_decay
```

```python
import jax
import jax.numpy as jnp
from jax import lax
from jax.experimental import pallas as pl
from jax.experimental.pallas import tpu as pltpu
from jax.sharding import PartitionSpec as P

SPAN = 64
SPANS = 8
TOK = 512
CHAN = 64
STATE = 128
LOCAL = 4
UPPER = 5
SHARDS = 32
ROWS = 16
GAIN_ROW = 2 * (UPPER + 1)
BLOCK = 128

NN = (((1,), (0,)), ((), ()))
NT = (((1,), (1,)), ((), ()))


def mm(left, right, dims=NN, precision=None):
    return lax.dot_general(
        left, right, dims, precision=precision, preferred_element_type=jnp.float32
    )


def split2(value):
    high = value.astype(jnp.bfloat16)
    return high, (value - high.astype(jnp.float32)).astype(jnp.bfloat16)


def split3(value):
    high, rest = split2(value)
    rest = value - high.astype(jnp.float32)
    return (high,) + split2(rest)


def iota(shape, axis):
    return lax.broadcasted_iota(jnp.int32, shape, axis)


def row_sums(row, keep):
    parts = [part.astype(jnp.float32) for part in split3(row)]
    stack = jnp.concatenate(parts + [jnp.zeros((5, row.shape[1]), jnp.float32)], 0)
    out = mm(stack.astype(jnp.bfloat16), keep)
    return out[0:1] + out[1:2] + out[2:3]


def states_kernel(x_ref, g_ref, b_ref, c_ref, gates_ref, decay_ref, starts_ref, msg_ref, rows_ref):
    keep = (iota((TOK, TOK), 0) <= iota((TOK, TOK), 1)).astype(jnp.float32).astype(jnp.bfloat16)
    run = row_sums(decay_ref[...], keep)
    last = run[:, TOK - 1 : TOK]
    token = iota((1, TOK), 1)
    counts = jnp.zeros((1, TOK), jnp.int32)
    total = jnp.int32(0)
    for span in range(SPANS):
        counts = counts + jnp.where(token >= span * SPAN, starts_ref[span], 0)
        total = total + starts_ref[span]
    entry = jnp.where(counts == 0, jnp.exp(run), 0.0)
    leave = jnp.where(counts == total, jnp.exp(last - run), 0.0)
    rows_ref[...] = jnp.concatenate(
        [run, counts.astype(jnp.float32), leave, entry, jnp.zeros((4, TOK), jnp.float32)], 0
    )
    keys, queries = b_ref[...], c_ref[...]
    inputs, grads = x_ref[...].astype(jnp.float32), g_ref[...].astype(jnp.float32)

    def put(place, value):
        for half in range(2):
            msg_ref[pl.ds(2 * place + half, SHARDS, stride=ROWS), :] = value[
                half * SHARDS : (half + 1) * SHARDS
            ]

    high, low = split2(inputs * leave)
    put(0, mm(high, keys) + mm(low, keys))
    for level in range(UPPER):
        high, low = split2(grads * (gates_ref[LOCAL + level : LOCAL + level + 1, :] * entry))
        put(1 + level, mm(high, queries) + mm(low, queries))
    msg_ref[pl.ds(GAIN_ROW, SHARDS, stride=ROWS), :] = jnp.broadcast_to(last, (SHARDS, STATE))
    for spare in range(GAIN_ROW + 1, ROWS):
        msg_ref[pl.ds(spare, SHARDS, stride=ROWS), :] = jnp.zeros((SHARDS, STATE), jnp.float32)


def chain_kernel(in_ref, out_ref):
    exact = lax.Precision.HIGHEST

    def get(row):
        return in_ref[pl.ds(row, SHARDS, stride=ROWS), :]

    def pair(place):
        return jnp.concatenate([get(2 * place), get(2 * place + 1)], 1)

    logs = get(GAIN_ROW)
    near = logs[:, :SHARDS]
    here, there = iota((SHARDS, SHARDS), 0), iota((SHARDS, SHARDS), 1)
    before = (there < here).astype(jnp.float32)
    after = (there > here).astype(jnp.float32)
    gain_before = jnp.exp(mm(before, jnp.where(here > there, near, 0.0), precision=exact))
    gain_after = jnp.exp(mm(after, jnp.where(here < there, near, 0.0), precision=exact))
    lanes = iota((SHARDS, 2 * STATE), 0)
    end_state = pair(0)
    picks = []
    for level in range(UPPER):
        block = (here >> (level + 1)) == (there >> (level + 1))
        early = ((there >> level) & 1) == 0
        picks.append(jnp.where(block & early & (there < here), gain_before, 0.0))
    prefix = mm(jnp.concatenate(picks, 0), end_state, precision=exact)
    returned = jnp.zeros((SHARDS, 2 * STATE), jnp.float32)
    gain_grad = jnp.zeros((SHARDS, 2 * STATE), jnp.float32)

    def put(place, value):
        for half in range(2):
            out_ref[pl.ds(2 * place + half, SHARDS, stride=ROWS), :] = value[
                :, half * STATE : (half + 1) * STATE
            ]

    for level in range(UPPER):
        block = (here >> (level + 1)) == (there >> (level + 1))
        late = ((there >> level) & 1) == 1
        pick = jnp.where(block & late & (there > here), gain_after, 0.0)
        suffix = mm(pick, pair(1 + level), precision=exact)
        front = prefix[level * SHARDS : (level + 1) * SHARDS]
        upper = ((lanes >> level) & 1) == 1
        put(1 + level, jnp.where(upper, front, 0.0))
        returned = returned + jnp.where(upper, 0.0, suffix)
        gain_grad = gain_grad + front * suffix
    put(0, returned)
    gain = (gain_grad[:, :STATE] + gain_grad[:, STATE:]) * jnp.exp(logs)
    out_ref[pl.ds(GAIN_ROW, SHARDS, stride=ROWS), :] = gain
    for spare in range(GAIN_ROW + 1, ROWS):
        out_ref[pl.ds(spare, SHARDS, stride=ROWS), :] = jnp.zeros((SHARDS, STATE), jnp.float32)


def within_kernel(
    x_ref, g_ref, b_ref, c_ref, gates_ref, rows_ref, vals_ref, keys_ref, queries_ref, sums_ref, flow_ref
):
    columns = jnp.transpose(rows_ref[...])
    run_col, count_col = columns[:, 0:1], columns[:, 1:2]
    x_t = jnp.transpose(x_ref[...].astype(jnp.float32)).astype(jnp.bfloat16)
    keys_t = jnp.transpose(b_ref[...].astype(jnp.float32)).astype(jnp.bfloat16)
    lane = iota((1, BLOCK), 1)
    causal = iota((BLOCK, BLOCK), 0) <= iota((BLOCK, BLOCK), 1)
    blocks = TOK // BLOCK
    for late in range(blocks):
        first, stop = late * BLOCK, (late + 1) * BLOCK
        queries, grads = c_ref[first:stop, :], g_ref[:, first:stop]
        run_row, count_row = rows_ref[0:1, first:stop], rows_ref[1:2, first:stop]
        gate_rows = [gates_ref[level : level + 1, first:stop] for level in range(LOCAL)]
        level_sums = [jnp.zeros((1, BLOCK), jnp.float32) for _ in range(LOCAL)]
        scores_all = mm(b_ref[:stop, :], queries, NT)
        kernel_grad_all = mm(x_t[:stop], grads)
        kernel_parts, grad_parts = [], []
        for early in range(late + 1):
            low, high = early * BLOCK, (early + 1) * BLOCK
            scores, kernel_grad = scores_all[low:high], kernel_grad_all[low:high]
            valid = count_row == count_col[low:high]
            if early == late:
                valid = valid & causal
            decay = jnp.where(valid, jnp.exp(jnp.minimum(run_row - run_col[low:high], 0.0)), 0.0)
            if early == late:
                top = jnp.where(lane < SPAN, gate_rows[0], gate_rows[1])
                gate = jnp.concatenate(
                    [
                        jnp.broadcast_to(top, (SPAN, BLOCK)),
                        jnp.broadcast_to(gate_rows[0], (SPAN, BLOCK)),
                    ],
                    0,
                )
            else:
                level = 1 + (late ^ early).bit_length()
                gate = gate_rows[level]
            weight = gate * decay
            kernel_parts.append((scores * weight).astype(jnp.bfloat16))
            score_grad = kernel_grad * weight
            grad_parts.append(score_grad.astype(jnp.bfloat16))
            terms = kernel_grad * scores * decay
            if early == late:
                upper = jnp.sum(terms[:SPAN], axis=0, keepdims=True)
                lower = jnp.sum(terms[SPAN:], axis=0, keepdims=True)
                level_sums[0] = level_sums[0] + jnp.where(lane < SPAN, upper, 0.0) + lower
                level_sums[1] = level_sums[1] + jnp.where(lane < SPAN, 0.0, upper)
                flow_ref[low:high, :] = score_grad * scores
            else:
                level_sums[level] = level_sums[level] + jnp.sum(terms, axis=0, keepdims=True)
                flow_ref[low:high, :] = flow_ref[low:high, :] + score_grad * scores
        kernel_low = jnp.concatenate(kernel_parts, 0)
        score_grad = jnp.concatenate(grad_parts, 0)
        vals = mm(grads, kernel_low, NT)
        key_part = mm(score_grad, queries)
        queries_ref[:, first:stop] = mm(keys_t[:, :stop], score_grad)
        vals_ref[:, first:stop] = vals[:, first:stop]
        keys_ref[first:stop, :] = key_part[first:stop]
        if late:
            vals_ref[:, :first] = vals_ref[:, :first] + vals[:, :first]
            keys_ref[:first, :] = keys_ref[:first, :] + key_part[:first]
        sums_ref[0:LOCAL, first:stop] = jnp.concatenate(level_sums, 0)
    ones = jnp.ones((8, BLOCK), jnp.bfloat16)
    column_flow = sum(mm(ones, part, NT) for part in split3(flow_ref[...]))
    sums_ref[LOCAL : 2 * LOCAL, :] = column_flow[0:LOCAL]


def cross_kernel(
    msg_ref,
    x_ref,
    g_ref,
    b_ref,
    c_ref,
    gates_ref,
    rows_ref,
    vals_ref,
    keys_ref,
    queries_ref,
    sums_ref,
    grad_inputs_ref,
    totals_ref,
    grad_gates_ref,
    grad_decay_ref,
):
    def get(place):
        return jnp.concatenate(
            [msg_ref[pl.ds(2 * place + half, SHARDS, stride=ROWS), :] for half in range(2)], 0
        )

    leave, entry = rows_ref[2:3, :], rows_ref[3:4, :]
    inputs, grads = x_ref[...].astype(jnp.float32), g_ref[...].astype(jnp.float32)
    keys, queries = b_ref[...], c_ref[...]

    returned = get(0)
    back_high, back_low = split2(returned)
    pulled = (mm(back_high, keys, NT) + mm(back_low, keys, NT)) * leave
    grad_inputs_ref[...] = (vals_ref[...] + pulled).astype(jnp.bfloat16)
    pulled_flow = jnp.sum(inputs * pulled, axis=0, keepdims=True)
    out_high, out_low = split2(jnp.transpose(inputs * leave))
    totals_ref[:, :STATE] = (
        keys_ref[...] + mm(out_high, back_high) + mm(out_high, back_low) + mm(out_low, back_high)
    )

    carried = jnp.concatenate([get(1 + level) for level in range(UPPER)], 0)
    front_high, front_low = split2(carried)
    turned_high, turned_low = split2(jnp.transpose(carried))
    seen = mm(front_high, queries, NT) + mm(front_low, queries, NT)
    scaled = []
    run_grad = -sums_ref[LOCAL : LOCAL + 1, :] - pulled_flow
    for level in range(LOCAL):
        gate_sum = sums_ref[level : level + 1, :]
        grad_gates_ref[level : level + 1, :] = gate_sum
        run_grad = run_grad + gates_ref[level : level + 1, :] * gate_sum
    for level in range(UPPER):
        row = slice(LOCAL + level, LOCAL + level + 1)
        gate = gates_ref[row, :]
        cross_value = jnp.sum(
            grads * seen[level * CHAN : (level + 1) * CHAN], axis=0, keepdims=True
        )
        grad_gate = entry * cross_value
        grad_gates_ref[row, :] = grad_gate
        run_grad = run_grad + gate * grad_gate
        scaled.append(grads * (gate * entry))
    in_high, in_low = split2(jnp.concatenate(scaled, 0))
    query_t = (
        queries_ref[...]
        + mm(turned_high, in_high)
        + mm(turned_low, in_high)
        + mm(turned_high, in_low)
    )
    totals_ref[:, STATE:] = jnp.transpose(query_t)

    gain = jnp.sum(msg_ref[pl.ds(GAIN_ROW, SHARDS, stride=ROWS), :], axis=0, keepdims=True)
    gain = jnp.sum(gain, axis=1, keepdims=True) + jnp.sum(pulled_flow, axis=1, keepdims=True)
    run_grad = run_grad + jnp.where(iota((1, TOK), 1) == TOK - 1, gain, 0.0)
    keep = (iota((TOK, TOK), 0) >= iota((TOK, TOK), 1)).astype(jnp.float32).astype(jnp.bfloat16)
    grad_decay_ref[...] = row_sums(run_grad, keep)


def f32(*shape):
    return jax.ShapeDtypeStruct(shape, jnp.float32)


def cost(flops, moved):
    return pl.CostEstimate(flops=flops, bytes_accessed=moved, transcendentals=0)


def local_states(inputs, grad_out, keys_b, queries_c, level_gates, log_decay, doc_starts):
    vmem = pl.BlockSpec(memory_space=pltpu.VMEM)
    return pl.pallas_call(
        states_kernel,
        out_shape=(f32(SHARDS * ROWS, STATE), f32(8, TOK)),
        in_specs=[vmem] * 6 + [pl.BlockSpec(memory_space=pltpu.SMEM)],
        out_specs=(vmem, vmem),
        cost_estimate=cost(100_000_000, 700_000),
        name="states",
    )(inputs, grad_out, keys_b, queries_c, level_gates, log_decay, doc_starts)


def chains(messages):
    return pl.pallas_call(
        chain_kernel, out_shape=f32(SHARDS * ROWS, STATE), cost_estimate=cost(20_000_000, 500_000), name="chains"
    )(messages)


def within_terms(inputs, grad_out, keys_b, queries_c, level_gates, rows):
    return pl.pallas_call(
        within_kernel,
        out_shape=(f32(CHAN, TOK), f32(TOK, STATE), f32(STATE, TOK), f32(2 * LOCAL, TOK)),
        scratch_shapes=[pltpu.VMEM((TOK, BLOCK), jnp.float32)],
        cost_estimate=cost(4_000_000_000, 1_000_000),
        name="within",
    )(inputs, grad_out, keys_b, queries_c, level_gates, rows)


def cross_terms(messages, inputs, grad_out, keys_b, queries_c, level_gates, rows, within):
    return pl.pallas_call(
        cross_kernel,
        out_shape=(
            jax.ShapeDtypeStruct((CHAN, TOK), jnp.bfloat16),
            f32(TOK, 2 * STATE),
            f32(LOCAL + UPPER, TOK),
            f32(1, TOK),
        ),
        cost_estimate=cost(300_000_000, 2_000_000),
        name="cross",
    )(messages, inputs, grad_out, keys_b, queries_c, level_gates, rows, *within)


def swap(messages):
    out = lax.all_to_all(messages.reshape(SHARDS, ROWS, STATE), "seq", 0, 0, tiled=True)
    return out.reshape(SHARDS * ROWS, STATE)


def shards(inputs, grad_out, keys_b, queries_c, level_gates, log_decay, doc_starts):
    messages, rows = local_states(
        inputs, grad_out, keys_b, queries_c, level_gates, log_decay, doc_starts
    )
    arrived = swap(messages)
    within = within_terms(inputs, grad_out, keys_b, queries_c, level_gates, rows)
    answers = swap(chains(arrived))
    grad_inputs, totals, grad_gates, grad_decay = cross_terms(
        answers, inputs, grad_out, keys_b, queries_c, level_gates, rows, within
    )
    heads = lax.axis_size("head")
    parts = lax.all_to_all(
        totals.reshape(heads, TOK // heads, 2 * STATE), "head", 0, 0, tiled=True
    )
    sums = jnp.sum(parts, axis=0).astype(jnp.bfloat16)
    return grad_inputs, sums[:, :STATE], sums[:, STATE:], grad_gates, grad_decay


def solution(mesh):
    by_head = P("head", "seq")
    in_specs = (by_head, by_head, P("seq", None), P("seq", None), by_head, by_head, P("seq"))
    out_specs = (by_head, P(("seq", "head"), None), P(("seq", "head"), None), by_head, by_head)
    return jax.shard_map(shards, mesh=mesh, in_specs=in_specs, out_specs=out_specs, check_vma=False)
```

```python
import jax
import jax.numpy as jnp
from jax import lax
from jax.experimental import pallas as pl
from jax.experimental.pallas import tpu as pltpu
from jax.sharding import PartitionSpec as P

SPAN = 64
SPANS = 8
TOK = 512
CHAN = 64
STATE = 128
LOCAL = 4
UPPER = 5
SHARDS = 32
ROWS = 16
GAIN_ROW = 2 * (UPPER + 1)
BLOCK = 128
PAIR = 2
CHUNK = 32
HALF = TOK // PAIR
LEND = 2 * CHAN + 8 + HALF // 2

NN = (((1,), (0,)), ((), ()))
NT = (((1,), (1,)), ((), ()))


def mm(left, right, dims=NN, precision=None):
    return lax.dot_general(
        left, right, dims, precision=precision, preferred_element_type=jnp.float32
    )


def split2(value):
    high = value.astype(jnp.bfloat16)
    return high, (value - high.astype(jnp.float32)).astype(jnp.bfloat16)


def split3(value):
    high, rest = split2(value)
    rest = value - high.astype(jnp.float32)
    return (high,) + split2(rest)


def iota(shape, axis):
    return lax.broadcasted_iota(jnp.int32, shape, axis)


def row_sums(row, keep):
    parts = [part.astype(jnp.float32) for part in split3(row)]
    stack = jnp.concatenate(parts + [jnp.zeros((5, row.shape[1]), jnp.float32)], 0)
    out = mm(stack.astype(jnp.bfloat16), keep)
    return out[0:1] + out[1:2] + out[2:3]


def states_kernel(x_ref, g_ref, b_ref, c_ref, gates_ref, decay_ref, starts_ref, msg_ref, rows_ref):
    keep = (iota((TOK, TOK), 0) <= iota((TOK, TOK), 1)).astype(jnp.float32).astype(jnp.bfloat16)
    run = row_sums(decay_ref[...], keep)
    last = run[:, TOK - 1 : TOK]
    token = iota((1, TOK), 1)
    counts = jnp.zeros((1, TOK), jnp.int32)
    total = jnp.int32(0)
    for span in range(SPANS):
        counts = counts + jnp.where(token >= span * SPAN, starts_ref[span], 0)
        total = total + starts_ref[span]
    entry = jnp.where(counts == 0, jnp.exp(run), 0.0)
    leave = jnp.where(counts == total, jnp.exp(last - run), 0.0)
    rows_ref[...] = jnp.concatenate(
        [run, counts.astype(jnp.float32), leave, entry, jnp.zeros((4, TOK), jnp.float32)], 0
    )
    keys, queries = b_ref[...], c_ref[...]
    inputs, grads = x_ref[...].astype(jnp.float32), g_ref[...].astype(jnp.float32)

    def put(place, value):
        for half in range(2):
            msg_ref[pl.ds(2 * place + half, SHARDS, stride=ROWS), :] = value[
                half * SHARDS : (half + 1) * SHARDS
            ]

    high, low = split2(inputs * leave)
    put(0, mm(high, keys) + mm(low, keys))
    for level in range(UPPER):
        high, low = split2(grads * (gates_ref[LOCAL + level : LOCAL + level + 1, :] * entry))
        put(1 + level, mm(high, queries) + mm(low, queries))
    msg_ref[pl.ds(GAIN_ROW, SHARDS, stride=ROWS), :] = jnp.broadcast_to(last, (SHARDS, STATE))
    for spare in range(GAIN_ROW + 1, ROWS):
        msg_ref[pl.ds(spare, SHARDS, stride=ROWS), :] = jnp.zeros((SHARDS, STATE), jnp.float32)


def chain_kernel(in_ref, order_ref, out_ref):
    del order_ref
    exact = lax.Precision.HIGHEST

    def send(row, value):
        for member in range(PAIR):
            out_ref[pl.ds(member * ROWS + row, SHARDS, stride=PAIR * ROWS), :] = value

    def get(row):
        return in_ref[pl.ds(row, SHARDS, stride=ROWS), :]

    def pair(place):
        return jnp.concatenate([get(2 * place), get(2 * place + 1)], 1)

    logs = get(GAIN_ROW)
    near = logs[:, :SHARDS]
    here, there = iota((SHARDS, SHARDS), 0), iota((SHARDS, SHARDS), 1)
    before = (there < here).astype(jnp.float32)
    after = (there > here).astype(jnp.float32)
    gain_before = jnp.exp(mm(before, jnp.where(here > there, near, 0.0), precision=exact))
    gain_after = jnp.exp(mm(after, jnp.where(here < there, near, 0.0), precision=exact))
    lanes = iota((SHARDS, 2 * STATE), 0)
    end_state = pair(0)
    picks = []
    for level in range(UPPER):
        block = (here >> (level + 1)) == (there >> (level + 1))
        early = ((there >> level) & 1) == 0
        picks.append(jnp.where(block & early & (there < here), gain_before, 0.0))
    prefix = mm(jnp.concatenate(picks, 0), end_state, precision=exact)
    returned = jnp.zeros((SHARDS, 2 * STATE), jnp.float32)
    gain_grad = jnp.zeros((SHARDS, 2 * STATE), jnp.float32)

    def put(place, value):
        for half in range(2):
            send(2 * place + half, value[:, half * STATE : (half + 1) * STATE])

    for level in range(UPPER):
        block = (here >> (level + 1)) == (there >> (level + 1))
        late = ((there >> level) & 1) == 1
        pick = jnp.where(block & late & (there > here), gain_after, 0.0)
        suffix = mm(pick, pair(1 + level), precision=exact)
        front = prefix[level * SHARDS : (level + 1) * SHARDS]
        upper = ((lanes >> level) & 1) == 1
        put(1 + level, jnp.where(upper, front, 0.0))
        returned = returned + jnp.where(upper, 0.0, suffix)
        gain_grad = gain_grad + front * suffix
    put(0, returned)
    gain = (gain_grad[:, :STATE] + gain_grad[:, STATE:]) * jnp.exp(logs)
    send(GAIN_ROW, gain)
    for spare in range(GAIN_ROW + 1, ROWS):
        send(spare, jnp.zeros((SHARDS, STATE), jnp.float32))


def chunk_rows(chunk, parity):
    return pl.ds(pl.multiple_of(chunk * PAIR * CHUNK + parity * CHUNK, CHUNK), CHUNK)


def within_kernel(
    side_ref,
    x_ref,
    g_ref,
    b_ref,
    c_ref,
    gates_ref,
    rows_ref,
    vals_ref,
    kept_ref,
    lend_ref,
    sums_ref,
    flow_ref,
    keys_ref,
    queries_ref,
    totals_ref,
):
    side = side_ref[0]
    lend_ref[0:CHAN, :] = x_ref[...].astype(jnp.float32) * rows_ref[2:3, :]
    lend_ref[CHAN : 2 * CHAN, :] = g_ref[...].astype(jnp.float32)
    lend_ref[2 * CHAN : 2 * CHAN + 8, :] = jnp.concatenate(
        [gates_ref[LOCAL:, :] * rows_ref[3:4, :], jnp.zeros((8 - UPPER, TOK), jnp.float32)], 0
    )
    columns = jnp.transpose(rows_ref[...])
    run_col, count_col = columns[:, 0:1], columns[:, 1:2]
    x_t = jnp.transpose(x_ref[...].astype(jnp.float32)).astype(jnp.bfloat16)
    keys_t = jnp.transpose(b_ref[...].astype(jnp.float32)).astype(jnp.bfloat16)
    lane = iota((1, BLOCK), 1)
    causal = iota((BLOCK, BLOCK), 0) <= iota((BLOCK, BLOCK), 1)
    blocks = TOK // BLOCK
    for late in range(blocks):
        first, stop = late * BLOCK, (late + 1) * BLOCK
        queries, grads = c_ref[first:stop, :], g_ref[:, first:stop]
        run_row, count_row = rows_ref[0:1, first:stop], rows_ref[1:2, first:stop]
        gate_rows = [gates_ref[level : level + 1, first:stop] for level in range(LOCAL)]
        level_sums = [jnp.zeros((1, BLOCK), jnp.float32) for _ in range(LOCAL)]
        scores_all = mm(b_ref[:stop, :], queries, NT)
        kernel_grad_all = mm(x_t[:stop], grads)
        kernel_parts, grad_parts = [], []
        for early in range(late + 1):
            low, high = early * BLOCK, (early + 1) * BLOCK
            scores, kernel_grad = scores_all[low:high], kernel_grad_all[low:high]
            valid = count_row == count_col[low:high]
            if early == late:
                valid = valid & causal
            decay = jnp.where(valid, jnp.exp(jnp.minimum(run_row - run_col[low:high], 0.0)), 0.0)
            if early == late:
                top = jnp.where(lane < SPAN, gate_rows[0], gate_rows[1])
                gate = jnp.concatenate(
                    [
                        jnp.broadcast_to(top, (SPAN, BLOCK)),
                        jnp.broadcast_to(gate_rows[0], (SPAN, BLOCK)),
                    ],
                    0,
                )
            else:
                level = 1 + (late ^ early).bit_length()
                gate = gate_rows[level]
            weight = gate * decay
            kernel_parts.append((scores * weight).astype(jnp.bfloat16))
            score_grad = kernel_grad * weight
            grad_parts.append(score_grad.astype(jnp.bfloat16))
            terms = kernel_grad * scores * decay
            if early == late:
                upper = jnp.sum(terms[:SPAN], axis=0, keepdims=True)
                lower = jnp.sum(terms[SPAN:], axis=0, keepdims=True)
                level_sums[0] = level_sums[0] + jnp.where(lane < SPAN, upper, 0.0) + lower
                level_sums[1] = level_sums[1] + jnp.where(lane < SPAN, 0.0, upper)
                flow_ref[low:high, :] = score_grad * scores
            else:
                level_sums[level] = level_sums[level] + jnp.sum(terms, axis=0, keepdims=True)
                flow_ref[low:high, :] = flow_ref[low:high, :] + score_grad * scores
        kernel_low = jnp.concatenate(kernel_parts, 0)
        score_grad = jnp.concatenate(grad_parts, 0)
        vals = mm(grads, kernel_low, NT)
        key_part = mm(score_grad, queries)
        queries_ref[:, first:stop] = mm(keys_t[:, :stop], score_grad)
        vals_ref[:, first:stop] = vals[:, first:stop]
        keys_ref[first:stop, :] = key_part[first:stop]
        if late:
            vals_ref[:, :first] = vals_ref[:, :first] + vals[:, :first]
            keys_ref[:first, :] = keys_ref[:first, :] + key_part[:first]
        sums_ref[0:LOCAL, first:stop] = jnp.concatenate(level_sums, 0)
    ones = jnp.ones((8, BLOCK), jnp.bfloat16)
    column_flow = sum(mm(ones, part, NT) for part in split3(flow_ref[...]))
    sums_ref[LOCAL : 2 * LOCAL, :] = column_flow[0:LOCAL]
    totals_ref[:, :STATE] = keys_ref[...]
    totals_ref[:, STATE:] = jnp.transpose(queries_ref[...])
    per_column = HALF // 2 // CHUNK
    for chunk in range(TOK // CHUNK // PAIR):
        kept_ref[chunk * CHUNK : (chunk + 1) * CHUNK, :] = totals_ref[chunk_rows(chunk, side), :]
        row = 2 * CHAN + 8 + chunk % per_column * CHUNK
        column = chunk // per_column * 2 * STATE
        lend_ref[row : row + CHUNK, column : column + 2 * STATE] = totals_ref[
            chunk_rows(chunk, 1 - side), :
        ]


def cross_kernel(
    side_ref,
    msg_ref,
    lent_ref,
    x_ref,
    g_ref,
    b_ref,
    c_ref,
    gates_ref,
    rows_ref,
    vals_ref,
    kept_ref,
    sums_ref,
    grad_inputs_ref,
    sent_ref,
    grad_gates_ref,
    grad_decay_ref,
    totals_ref,
):
    side = side_ref[0]
    first_side = side == 0

    def load(row, member):
        return msg_ref[pl.ds(member * ROWS + row, SHARDS, stride=PAIR * ROWS), :]

    def get(place):
        mine, other = [], []
        for half in range(2):
            even, odd = load(2 * place + half, 0), load(2 * place + half, 1)
            mine.append(jnp.where(first_side, even, odd))
            other.append(jnp.where(first_side, odd, even))
        return jnp.concatenate(mine, 0), jnp.concatenate(other, 0)

    leave, entry = rows_ref[2:3, :], rows_ref[3:4, :]
    inputs, grads = x_ref[...].astype(jnp.float32), g_ref[...].astype(jnp.float32)
    keys, queries = b_ref[...], c_ref[...]

    returned, returned_other = get(0)
    back_high, back_low = split2(returned)
    pulled = (mm(back_high, keys, NT) + mm(back_low, keys, NT)) * leave
    grad_inputs_ref[...] = (vals_ref[...] + pulled).astype(jnp.bfloat16)
    pulled_flow = jnp.sum(inputs * pulled, axis=0, keepdims=True)
    other_high, other_low = split2(returned_other)
    both_high = jnp.concatenate([back_high, other_high], 0)
    both_low = jnp.concatenate([back_low, other_low], 0)
    out_high, out_low = split2(
        jnp.transpose(jnp.concatenate([inputs * leave, lent_ref[0:CHAN, :]], 0))
    )
    totals_ref[:, :STATE] = mm(out_high, both_high) + mm(out_high, both_low) + mm(out_low, both_high)

    states = [get(1 + level) for level in range(UPPER)]
    carried = jnp.concatenate([pair[0] for pair in states], 0)
    carried_other = jnp.concatenate([pair[1] for pair in states], 0)
    front_high, front_low = split2(carried)
    turned_high, turned_low = split2(
        jnp.transpose(jnp.concatenate([carried, carried_other], 0))
    )
    seen = mm(front_high, queries, NT) + mm(front_low, queries, NT)
    scaled = []
    run_grad = -sums_ref[LOCAL : LOCAL + 1, :] - pulled_flow
    for level in range(LOCAL):
        gate_sum = sums_ref[level : level + 1, :]
        grad_gates_ref[level : level + 1, :] = gate_sum
        run_grad = run_grad + gates_ref[level : level + 1, :] * gate_sum
    for level in range(UPPER):
        row = slice(LOCAL + level, LOCAL + level + 1)
        gate = gates_ref[row, :]
        cross_value = jnp.sum(
            grads * seen[level * CHAN : (level + 1) * CHAN], axis=0, keepdims=True
        )
        grad_gate = entry * cross_value
        grad_gates_ref[row, :] = grad_gate
        run_grad = run_grad + gate * grad_gate
        scaled.append(grads * (gate * entry))
    lent_grads = lent_ref[CHAN : 2 * CHAN, :]
    for level in range(UPPER):
        scaled.append(lent_grads * lent_ref[2 * CHAN + level : 2 * CHAN + level + 1, :])
    in_high, in_low = split2(jnp.concatenate(scaled, 0))
    query_t = mm(turned_high, in_high) + mm(turned_low, in_high) + mm(turned_high, in_low)
    totals_ref[:, STATE:] = jnp.transpose(query_t)
    per_column = HALF // 2 // CHUNK
    for chunk in range(TOK // CHUNK // PAIR):
        place = slice(chunk * CHUNK, (chunk + 1) * CHUNK)
        row = 2 * CHAN + 8 + chunk % per_column * CHUNK
        column = chunk // per_column * 2 * STATE
        sent_ref[place, :] = (
            totals_ref[chunk_rows(chunk, side), :]
            + kept_ref[place, :]
            + lent_ref[row : row + CHUNK, column : column + 2 * STATE]
        )

    gain = jnp.where(first_side, load(GAIN_ROW, 0), load(GAIN_ROW, 1))
    gain = jnp.sum(gain, axis=0, keepdims=True)
    gain = jnp.sum(gain, axis=1, keepdims=True) + jnp.sum(pulled_flow, axis=1, keepdims=True)
    run_grad = run_grad + jnp.where(iota((1, TOK), 1) == TOK - 1, gain, 0.0)
    keep = (iota((TOK, TOK), 0) >= iota((TOK, TOK), 1)).astype(jnp.float32).astype(jnp.bfloat16)
    grad_decay_ref[...] = row_sums(run_grad, keep)


def f32(*shape):
    return jax.ShapeDtypeStruct(shape, jnp.float32)


def cost(flops, moved):
    return pl.CostEstimate(flops=flops, bytes_accessed=moved, transcendentals=0)


def local_states(inputs, grad_out, keys_b, queries_c, level_gates, log_decay, doc_starts):
    vmem = pl.BlockSpec(memory_space=pltpu.VMEM)
    return pl.pallas_call(
        states_kernel,
        out_shape=(f32(SHARDS * ROWS, STATE), f32(8, TOK)),
        in_specs=[vmem] * 6 + [pl.BlockSpec(memory_space=pltpu.SMEM)],
        out_specs=(vmem, vmem),
        cost_estimate=cost(100_000_000, 700_000),
        name="states",
    )(inputs, grad_out, keys_b, queries_c, level_gates, log_decay, doc_starts)


def chains(messages, order):
    return pl.pallas_call(
        chain_kernel,
        out_shape=f32(PAIR * SHARDS * ROWS, STATE),
        in_specs=[pl.BlockSpec(memory_space=pltpu.VMEM), pl.BlockSpec(memory_space=pl.ANY)],
        cost_estimate=cost(20_000_000, 800_000),
        name="chains",
    )(messages, order)


def within_terms(side, inputs, grad_out, keys_b, queries_c, level_gates, rows):
    vmem = pl.BlockSpec(memory_space=pltpu.VMEM)
    return pl.pallas_call(
        within_kernel,
        out_shape=(f32(CHAN, TOK), f32(HALF, 2 * STATE), f32(LEND, TOK), f32(2 * LOCAL, TOK)),
        in_specs=[pl.BlockSpec(memory_space=pltpu.SMEM)] + [vmem] * 6,
        scratch_shapes=[
            pltpu.VMEM((TOK, BLOCK), jnp.float32),
            pltpu.VMEM((TOK, STATE), jnp.float32),
            pltpu.VMEM((STATE, TOK), jnp.float32),
            pltpu.VMEM((TOK, 2 * STATE), jnp.float32),
        ],
        cost_estimate=cost(4_000_000_000, 2_000_000),
        name="within",
    )(side, inputs, grad_out, keys_b, queries_c, level_gates, rows)


def cross_terms(side, messages, lent, inputs, grad_out, keys_b, queries_c, level_gates, rows, vals, kept, sums):
    vmem = pl.BlockSpec(memory_space=pltpu.VMEM)
    return pl.pallas_call(
        cross_kernel,
        out_shape=(
            jax.ShapeDtypeStruct((CHAN, TOK), jnp.bfloat16),
            f32(HALF, 2 * STATE),
            f32(LOCAL + UPPER, TOK),
            f32(1, TOK),
        ),
        in_specs=[pl.BlockSpec(memory_space=pltpu.SMEM)] + [vmem] * 11,
        scratch_shapes=[pltpu.VMEM((TOK, 2 * STATE), jnp.float32)],
        cost_estimate=cost(600_000_000, 3_000_000),
        name="cross",
    )(side, messages, lent, inputs, grad_out, keys_b, queries_c, level_gates, rows, vals, kept, sums)


def shards(inputs, grad_out, keys_b, queries_c, level_gates, log_decay, doc_starts):
    heads = lax.axis_size("head")
    side = (lax.axis_index("head") % PAIR).astype(jnp.int32).reshape(1)
    messages, rows = local_states(
        inputs, grad_out, keys_b, queries_c, level_gates, log_decay, doc_starts
    )
    arrived = lax.all_to_all(messages.reshape(SHARDS, ROWS, STATE), "seq", 0, 0, tiled=True)
    vals, kept, lend, sums = within_terms(
        side, inputs, grad_out, keys_b, queries_c, level_gates, rows
    )
    lent = lax.ppermute(lend, "head", [(head, head ^ 1) for head in range(heads)])
    answers = chains(arrived.reshape(SHARDS * ROWS, STATE), sums)
    pairs = [
        [shard * heads + head + member for shard in range(SHARDS) for member in range(PAIR)]
        for head in range(0, heads, PAIR)
    ]
    answers = lax.all_to_all(
        answers.reshape(PAIR * SHARDS, ROWS, STATE),
        ("seq", "head"),
        0,
        0,
        axis_index_groups=pairs,
        tiled=True,
    ).reshape(PAIR * SHARDS * ROWS, STATE)
    grad_inputs, totals, grad_gates, grad_decay = cross_terms(
        side, answers, lent, inputs, grad_out, keys_b, queries_c, level_gates, rows, vals, kept, sums
    )
    sides = [list(range(start, heads, PAIR)) for start in range(PAIR)]
    parts = lax.all_to_all(
        totals.reshape(heads // PAIR, CHUNK, 2 * STATE),
        "head",
        0,
        0,
        axis_index_groups=sides,
        tiled=True,
    )
    total = jnp.sum(parts, axis=0).astype(jnp.bfloat16)
    return grad_inputs, total[:, :STATE], total[:, STATE:], grad_gates, grad_decay


def solution(mesh):
    by_head = P("head", "seq")
    in_specs = (by_head, by_head, P("seq", None), P("seq", None), by_head, by_head, P("seq"))
    out_specs = (by_head, P(("seq", "head"), None), P(("seq", "head"), None), by_head, by_head)
    return jax.shard_map(shards, mesh=mesh, in_specs=in_specs, out_specs=out_specs, check_vma=False)
```

```python
import jax
import jax.numpy as jnp
from jax import lax
from jax.experimental import pallas as pl
from jax.experimental.pallas import tpu as pltpu
from jax.sharding import PartitionSpec as P

SPAN = 64
SPANS = 8
TOK = 512
CHAN = 64
STATE = 128
LOCAL = 4
UPPER = 5
SHARDS = 32
ROWS = 16
GAIN_ROW = 2 * (UPPER + 1)
BLOCK = 128

NN = (((1,), (0,)), ((), ()))
NT = (((1,), (1,)), ((), ()))


def mm(left, right, dims=NN, precision=None):
    return lax.dot_general(
        left, right, dims, precision=precision, preferred_element_type=jnp.float32
    )


def split2(value):
    high = value.astype(jnp.bfloat16)
    return high, (value - high.astype(jnp.float32)).astype(jnp.bfloat16)


def mm_split(left, right):
    left_high, left_low = split2(left)
    right_high, right_low = split2(right)
    return mm(left_high, right_high) + mm(left_high, right_low) + mm(left_low, right_high)


def split3(value):
    high, rest = split2(value)
    rest = value - high.astype(jnp.float32)
    return (high,) + split2(rest)


def iota(shape, axis):
    return lax.broadcasted_iota(jnp.int32, shape, axis)


def row_sums(row, backward=False):
    blocks = TOK // BLOCK
    stack = jnp.concatenate([row[:, at * BLOCK : (at + 1) * BLOCK] for at in range(blocks)], 0)
    parts = [part.astype(jnp.float32) for part in split3(stack)]
    parts.append(jnp.zeros((16 - 3 * blocks, BLOCK), jnp.float32))
    here, there = iota((BLOCK, BLOCK), 0), iota((BLOCK, BLOCK), 1)
    keep = (here >= there if backward else here <= there).astype(jnp.float32)
    out = mm(jnp.concatenate(parts, 0).astype(jnp.bfloat16), keep.astype(jnp.bfloat16))
    sums = out[0:blocks] + out[blocks : 2 * blocks] + out[2 * blocks : 3 * blocks]
    offset = jnp.zeros((1, 1), jnp.float32)
    pieces = []
    for at in range(blocks - 1, -1, -1) if backward else range(blocks):
        piece = sums[at : at + 1] + offset
        offset = piece[:, :1] if backward else piece[:, BLOCK - 1 :]
        pieces.append(piece)
    return jnp.concatenate(pieces[::-1] if backward else pieces, 1)


def states_kernel(x_ref, g_ref, b_ref, c_ref, gates_ref, decay_ref, starts_ref, msg_ref, rows_ref):
    run = row_sums(decay_ref[...])
    last = run[:, TOK - 1 : TOK]
    token = iota((1, TOK), 1)
    counts = jnp.zeros((1, TOK), jnp.int32)
    total = jnp.int32(0)
    for span in range(SPANS):
        counts = counts + jnp.where(token >= span * SPAN, starts_ref[span], 0)
        total = total + starts_ref[span]
    entry = jnp.where(counts == 0, jnp.exp(run), 0.0)
    leave = jnp.where(counts == total, jnp.exp(last - run), 0.0)
    rows_ref[...] = jnp.concatenate(
        [run, counts.astype(jnp.float32), leave, entry, jnp.zeros((4, TOK), jnp.float32)], 0
    )
    keys, queries = b_ref[...], c_ref[...]
    inputs, grads = x_ref[...].astype(jnp.float32), g_ref[...].astype(jnp.float32)

    def put(place, value):
        for half in range(2):
            msg_ref[pl.ds(2 * place + half, SHARDS, stride=ROWS), :] = value[
                half * SHARDS : (half + 1) * SHARDS
            ]

    high, low = split2(inputs * leave)
    put(0, mm(high, keys) + mm(low, keys))
    for level in range(UPPER):
        high, low = split2(grads * (gates_ref[LOCAL + level : LOCAL + level + 1, :] * entry))
        put(1 + level, mm(high, queries) + mm(low, queries))
    msg_ref[pl.ds(GAIN_ROW, SHARDS, stride=ROWS), :] = jnp.broadcast_to(last, (SHARDS, STATE))
    for spare in range(GAIN_ROW + 1, ROWS):
        msg_ref[pl.ds(spare, SHARDS, stride=ROWS), :] = jnp.zeros((SHARDS, STATE), jnp.float32)


def chain_kernel(in_ref, out_ref):
    def get(row):
        return in_ref[pl.ds(row, SHARDS, stride=ROWS), :]

    def pair(place):
        return jnp.concatenate([get(2 * place), get(2 * place + 1)], 1)

    logs = get(GAIN_ROW)
    near = logs[:, :SHARDS]
    here, there = iota((SHARDS, SHARDS), 0), iota((SHARDS, SHARDS), 1)
    before = (there < here).astype(jnp.float32).astype(jnp.bfloat16)
    after = (there > here).astype(jnp.float32).astype(jnp.bfloat16)
    gain_before = jnp.exp(sum(mm(before, part) for part in split3(jnp.where(here > there, near, 0.0))))
    gain_after = jnp.exp(sum(mm(after, part) for part in split3(jnp.where(here < there, near, 0.0))))
    lanes = iota((SHARDS, 2 * STATE), 0)
    end_state = pair(0)
    picks = []
    for level in range(UPPER):
        block = (here >> (level + 1)) == (there >> (level + 1))
        early = ((there >> level) & 1) == 0
        picks.append(jnp.where(block & early & (there < here), gain_before, 0.0))
    prefix = mm_split(jnp.concatenate(picks, 0), end_state)
    returned = jnp.zeros((SHARDS, 2 * STATE), jnp.float32)
    gain_grad = jnp.zeros((SHARDS, 2 * STATE), jnp.float32)

    def put(place, value):
        for half in range(2):
            out_ref[pl.ds(2 * place + half, SHARDS, stride=ROWS), :] = value[
                :, half * STATE : (half + 1) * STATE
            ]

    for level in range(UPPER):
        block = (here >> (level + 1)) == (there >> (level + 1))
        late = ((there >> level) & 1) == 1
        pick = jnp.where(block & late & (there > here), gain_after, 0.0)
        suffix = mm_split(pick, pair(1 + level))
        front = prefix[level * SHARDS : (level + 1) * SHARDS]
        upper = ((lanes >> level) & 1) == 1
        put(1 + level, jnp.where(upper, front, 0.0))
        returned = returned + jnp.where(upper, 0.0, suffix)
        gain_grad = gain_grad + front * suffix
    put(0, returned)
    gain = (gain_grad[:, :STATE] + gain_grad[:, STATE:]) * jnp.exp(logs)
    out_ref[pl.ds(GAIN_ROW, SHARDS, stride=ROWS), :] = gain
    for spare in range(GAIN_ROW + 1, ROWS):
        out_ref[pl.ds(spare, SHARDS, stride=ROWS), :] = jnp.zeros((SHARDS, STATE), jnp.float32)


def within_kernel(
    x_ref,
    g_ref,
    b_ref,
    c_ref,
    gates_ref,
    rows_ref,
    vals_ref,
    totals_ref,
    sums_ref,
    x_high_ref,
    x_low_ref,
    g_high_ref,
    g_low_ref,
    flow_ref,
    keys_ref,
    queries_ref,
):
    x_high_ref[...], x_low_ref[...] = split2(
        jnp.transpose(x_ref[...].astype(jnp.float32) * rows_ref[2:3, :])
    )
    grads_wide = g_ref[...].astype(jnp.float32)
    scaled = [
        grads_wide * (gates_ref[level : level + 1, :] * rows_ref[3:4, :])
        for level in range(LOCAL, LOCAL + UPPER)
    ]
    g_high_ref[...], g_low_ref[...] = split2(jnp.transpose(jnp.concatenate(scaled, 0)))
    columns = jnp.transpose(rows_ref[...])
    run_col, count_col = columns[:, 0:1], columns[:, 1:2]
    x_t = jnp.transpose(x_ref[...].astype(jnp.float32)).astype(jnp.bfloat16)
    keys_t = jnp.transpose(b_ref[...].astype(jnp.float32)).astype(jnp.bfloat16)
    lane = iota((1, BLOCK), 1)
    causal = iota((BLOCK, BLOCK), 0) <= iota((BLOCK, BLOCK), 1)
    blocks = TOK // BLOCK
    for late in range(blocks):
        first, stop = late * BLOCK, (late + 1) * BLOCK
        queries, grads = c_ref[first:stop, :], g_ref[:, first:stop]
        run_row, count_row = rows_ref[0:1, first:stop], rows_ref[1:2, first:stop]
        gate_rows = [gates_ref[level : level + 1, first:stop] for level in range(LOCAL)]
        level_sums = [jnp.zeros((1, BLOCK), jnp.float32) for _ in range(LOCAL)]
        scores_all = mm(b_ref[:stop, :], queries, NT)
        kernel_grad_all = mm(x_t[:stop], grads)
        kernel_parts, grad_parts = [], []
        for early in range(late + 1):
            low, high = early * BLOCK, (early + 1) * BLOCK
            scores, kernel_grad = scores_all[low:high], kernel_grad_all[low:high]
            valid = count_row == count_col[low:high]
            if early == late:
                valid = valid & causal
            decay = jnp.where(valid, jnp.exp(jnp.minimum(run_row - run_col[low:high], 0.0)), 0.0)
            if early == late:
                top = jnp.where(lane < SPAN, gate_rows[0], gate_rows[1])
                gate = jnp.concatenate(
                    [
                        jnp.broadcast_to(top, (SPAN, BLOCK)),
                        jnp.broadcast_to(gate_rows[0], (SPAN, BLOCK)),
                    ],
                    0,
                )
            else:
                level = 1 + (late ^ early).bit_length()
                gate = gate_rows[level]
            weight = gate * decay
            kernel_parts.append((scores * weight).astype(jnp.bfloat16))
            score_grad = kernel_grad * weight
            grad_parts.append(score_grad.astype(jnp.bfloat16))
            terms = kernel_grad * scores * decay
            if early == late:
                upper = jnp.sum(terms[:SPAN], axis=0, keepdims=True)
                lower = jnp.sum(terms[SPAN:], axis=0, keepdims=True)
                level_sums[0] = level_sums[0] + jnp.where(lane < SPAN, upper, 0.0) + lower
                level_sums[1] = level_sums[1] + jnp.where(lane < SPAN, 0.0, upper)
                flow_ref[low:high, :] = score_grad * scores
            else:
                level_sums[level] = level_sums[level] + jnp.sum(terms, axis=0, keepdims=True)
                flow_ref[low:high, :] = flow_ref[low:high, :] + score_grad * scores
        kernel_low = jnp.concatenate(kernel_parts, 0)
        score_grad = jnp.concatenate(grad_parts, 0)
        vals = mm(grads, kernel_low, NT)
        key_part = mm(score_grad, queries)
        queries_ref[:, first:stop] = mm(keys_t[:, :stop], score_grad)
        vals_ref[:, first:stop] = vals[:, first:stop]
        keys_ref[first:stop, :] = key_part[first:stop]
        if late:
            vals_ref[:, :first] = vals_ref[:, :first] + vals[:, :first]
            keys_ref[:first, :] = keys_ref[:first, :] + key_part[:first]
        sums_ref[0:LOCAL, first:stop] = jnp.concatenate(level_sums, 0)
    ones = jnp.ones((8, BLOCK), jnp.bfloat16)
    column_flow = sum(mm(ones, part, NT) for part in split3(flow_ref[...]))
    sums_ref[LOCAL : 2 * LOCAL, :] = column_flow[0:LOCAL]
    totals_ref[:, :STATE] = keys_ref[...]
    totals_ref[:, STATE:] = jnp.transpose(queries_ref[...])


def cross_kernel(
    msg_ref,
    x_ref,
    g_ref,
    b_ref,
    c_ref,
    gates_ref,
    rows_ref,
    vals_ref,
    within_ref,
    sums_ref,
    x_high_ref,
    x_low_ref,
    g_high_ref,
    g_low_ref,
    grad_inputs_ref,
    totals_ref,
    grad_gates_ref,
    grad_decay_ref,
):
    def get(place):
        return jnp.concatenate(
            [msg_ref[pl.ds(2 * place + half, SHARDS, stride=ROWS), :] for half in range(2)], 0
        )

    leave, entry = rows_ref[2:3, :], rows_ref[3:4, :]
    inputs, grads = x_ref[...].astype(jnp.float32), g_ref[...].astype(jnp.float32)
    keys, queries = b_ref[...], c_ref[...]

    returned = get(0)
    back_high, back_low = split2(returned)
    pulled = (mm(back_high, keys, NT) + mm(back_low, keys, NT)) * leave
    grad_inputs_ref[...] = (vals_ref[...] + pulled).astype(jnp.bfloat16)
    pulled_flow = jnp.sum(inputs * pulled, axis=0, keepdims=True)
    totals_ref[:, :STATE] = (
        within_ref[:, :STATE]
        + mm(x_high_ref[...], back_high)
        + mm(x_high_ref[...], back_low)
        + mm(x_low_ref[...], back_high)
    )

    carried = jnp.concatenate([get(1 + level) for level in range(UPPER)], 0)
    front_high, front_low = split2(carried)
    totals_ref[:, STATE:] = (
        within_ref[:, STATE:]
        + mm(g_high_ref[...], front_high)
        + mm(g_high_ref[...], front_low)
        + mm(g_low_ref[...], front_high)
    )
    seen = mm(front_high, queries, NT) + mm(front_low, queries, NT)
    run_grad = -sums_ref[LOCAL : LOCAL + 1, :] - pulled_flow
    for level in range(LOCAL):
        gate_sum = sums_ref[level : level + 1, :]
        grad_gates_ref[level : level + 1, :] = gate_sum
        run_grad = run_grad + gates_ref[level : level + 1, :] * gate_sum
    for level in range(UPPER):
        row = slice(LOCAL + level, LOCAL + level + 1)
        gate = gates_ref[row, :]
        cross_value = jnp.sum(
            grads * seen[level * CHAN : (level + 1) * CHAN], axis=0, keepdims=True
        )
        grad_gate = entry * cross_value
        grad_gates_ref[row, :] = grad_gate
        run_grad = run_grad + gate * grad_gate

    gain = jnp.sum(msg_ref[pl.ds(GAIN_ROW, SHARDS, stride=ROWS), :], axis=0, keepdims=True)
    gain = jnp.sum(gain, axis=1, keepdims=True) + jnp.sum(pulled_flow, axis=1, keepdims=True)
    run_grad = run_grad + jnp.where(iota((1, TOK), 1) == TOK - 1, gain, 0.0)
    grad_decay_ref[...] = row_sums(run_grad, backward=True)


def f32(*shape):
    return jax.ShapeDtypeStruct(shape, jnp.float32)


def near(*shape, dtype=jnp.float32):
    return pltpu.VMEM(shape, dtype)


def hold(value):
    return pltpu.with_memory_space_constraint(value, pltpu.VMEM)


def low(*shape):
    return jax.ShapeDtypeStruct(shape, jnp.bfloat16)


def cost(flops, moved):
    return pl.CostEstimate(flops=flops, bytes_accessed=moved, transcendentals=0)


def local_states(inputs, grad_out, keys_b, queries_c, level_gates, log_decay, doc_starts):
    vmem = pl.BlockSpec(memory_space=pltpu.VMEM)
    return pl.pallas_call(
        states_kernel,
        out_shape=(near(SHARDS * ROWS, STATE), near(8, TOK)),
        in_specs=[vmem] * 6 + [pl.BlockSpec(memory_space=pltpu.SMEM)],
        out_specs=(vmem, vmem),
        cost_estimate=cost(100_000_000, 700_000),
        name="states",
    )(inputs, grad_out, keys_b, queries_c, level_gates, log_decay, doc_starts)


def chains(messages):
    return pl.pallas_call(
        chain_kernel,
        out_shape=near(SHARDS * ROWS, STATE),
        in_specs=[pl.BlockSpec(memory_space=pltpu.VMEM)],
        out_specs=pl.BlockSpec(memory_space=pltpu.VMEM),
        cost_estimate=cost(20_000_000, 500_000),
        name="chains",
    )(hold(messages))


def within_terms(inputs, grad_out, keys_b, queries_c, level_gates, rows):
    vmem = pl.BlockSpec(memory_space=pltpu.VMEM)
    return pl.pallas_call(
        within_kernel,
        out_shape=(
            near(CHAN, TOK),
            near(TOK, 2 * STATE),
            near(2 * LOCAL, TOK),
            near(TOK, CHAN, dtype=jnp.bfloat16),
            near(TOK, CHAN, dtype=jnp.bfloat16),
            near(TOK, UPPER * CHAN, dtype=jnp.bfloat16),
            near(TOK, UPPER * CHAN, dtype=jnp.bfloat16),
        ),
        in_specs=[vmem] * 6,
        out_specs=(vmem,) * 7,
        scratch_shapes=[
            pltpu.VMEM((TOK, BLOCK), jnp.float32),
            pltpu.VMEM((TOK, STATE), jnp.float32),
            pltpu.VMEM((STATE, TOK), jnp.float32),
        ],
        cost_estimate=cost(4_000_000_000, 1_000_000),
        name="within",
    )(*[hold(part) for part in (inputs, grad_out, keys_b, queries_c, level_gates, rows)])


def cross_terms(messages, inputs, grad_out, keys_b, queries_c, level_gates, rows, within):
    vmem = pl.BlockSpec(memory_space=pltpu.VMEM)
    return pl.pallas_call(
        cross_kernel,
        out_shape=(
            low(CHAN, TOK),
            near(TOK, 2 * STATE),
            f32(LOCAL + UPPER, TOK),
            f32(1, TOK),
        ),
        in_specs=[vmem] * 14,
        out_specs=(vmem,) * 4,
        cost_estimate=cost(300_000_000, 2_000_000),
        name="cross",
    )(
        *[
            hold(part)
            for part in (messages, inputs, grad_out, keys_b, queries_c, level_gates, rows, *within)
        ]
    )


def swap(messages):
    out = lax.all_to_all(messages.reshape(SHARDS, ROWS, STATE), "seq", 0, 0, tiled=True)
    return out.reshape(SHARDS * ROWS, STATE)


def shards(inputs, grad_out, keys_b, queries_c, level_gates, log_decay, doc_starts):
    messages, rows = local_states(
        inputs, grad_out, keys_b, queries_c, level_gates, log_decay, doc_starts
    )
    arrived = swap(messages)
    within = within_terms(inputs, grad_out, keys_b, queries_c, level_gates, rows)
    answers = swap(chains(arrived))
    grad_inputs, totals, grad_gates, grad_decay = cross_terms(
        answers, inputs, grad_out, keys_b, queries_c, level_gates, rows, within
    )
    heads = lax.axis_size("head")
    parts = lax.all_to_all(
        totals.reshape(heads, TOK // heads, 2 * STATE), "head", 0, 0, tiled=True
    )
    sums = jnp.sum(parts, axis=0).astype(jnp.bfloat16)
    return grad_inputs, sums[:, :STATE], sums[:, STATE:], grad_gates, grad_decay


def solution(mesh):
    by_head = P("head", "seq")
    in_specs = (by_head, by_head, P("seq", None), P("seq", None), by_head, by_head, P("seq"))
    out_specs = (by_head, P(("seq", "head"), None), P(("seq", "head"), None), by_head, by_head)
    return jax.shard_map(shards, mesh=mesh, in_specs=in_specs, out_specs=out_specs, check_vma=False)
```

```python
import jax
import jax.numpy as jnp
from jax import lax
from jax.experimental import pallas as pl
from jax.experimental.pallas import tpu as pltpu
from jax.sharding import PartitionSpec as P

SPAN = 64
SPANS = 8
TOK = 512
CHAN = 64
STATE = 128
LOCAL = 4
UPPER = 5
SHARDS = 32
ROWS = 16
GAIN_ROW = 2 * (UPPER + 1)
BLOCK = 128
PAIR = 2
CHUNK = 32
HALF = TOK // PAIR
LENT_ROWS = 2 * CHAN
LENT_GATES = LENT_ROWS + 8
LEND = LENT_GATES + 16

NN = (((1,), (0,)), ((), ()))
NT = (((1,), (1,)), ((), ()))


def mm(left, right, dims=NN, precision=None):
    return lax.dot_general(
        left, right, dims, precision=precision, preferred_element_type=jnp.float32
    )


def split2(value):
    high = value.astype(jnp.bfloat16)
    return high, (value - high.astype(jnp.float32)).astype(jnp.bfloat16)


def mm_split(left, right):
    left_high, left_low = split2(left)
    right_high, right_low = split2(right)
    return mm(left_high, right_high) + mm(left_high, right_low) + mm(left_low, right_high)


def split3(value):
    high, rest = split2(value)
    rest = value - high.astype(jnp.float32)
    return (high,) + split2(rest)


def iota(shape, axis):
    return lax.broadcasted_iota(jnp.int32, shape, axis)


def row_sums(row, backward=False):
    blocks = TOK // BLOCK
    stack = jnp.concatenate([row[:, at * BLOCK : (at + 1) * BLOCK] for at in range(blocks)], 0)
    parts = [part.astype(jnp.float32) for part in split3(stack)]
    parts.append(jnp.zeros((16 - 3 * blocks, BLOCK), jnp.float32))
    here, there = iota((BLOCK, BLOCK), 0), iota((BLOCK, BLOCK), 1)
    keep = (here >= there if backward else here <= there).astype(jnp.float32)
    out = mm(jnp.concatenate(parts, 0).astype(jnp.bfloat16), keep.astype(jnp.bfloat16))
    sums = out[0:blocks] + out[blocks : 2 * blocks] + out[2 * blocks : 3 * blocks]
    offset = jnp.zeros((1, 1), jnp.float32)
    pieces = []
    for at in range(blocks - 1, -1, -1) if backward else range(blocks):
        piece = sums[at : at + 1] + offset
        offset = piece[:, :1] if backward else piece[:, BLOCK - 1 :]
        pieces.append(piece)
    return jnp.concatenate(pieces[::-1] if backward else pieces, 1)


def states_kernel(x_ref, g_ref, b_ref, c_ref, gates_ref, decay_ref, starts_ref, msg_ref, rows_ref, lend_ref):
    run = row_sums(decay_ref[...])
    last = run[:, TOK - 1 : TOK]
    token = iota((1, TOK), 1)
    counts = jnp.zeros((1, TOK), jnp.int32)
    total = jnp.int32(0)
    for span in range(SPANS):
        counts = counts + jnp.where(token >= span * SPAN, starts_ref[span], 0)
        total = total + starts_ref[span]
    entry = jnp.where(counts == 0, jnp.exp(run), 0.0)
    leave = jnp.where(counts == total, jnp.exp(last - run), 0.0)
    rows = jnp.concatenate(
        [run, counts.astype(jnp.float32), leave, entry, jnp.zeros((4, TOK), jnp.float32)], 0
    )
    rows_ref[...] = rows
    lend_ref[LENT_ROWS:LENT_GATES, :] = rows
    lend_ref[LENT_GATES:, :] = jnp.concatenate(
        [gates_ref[...], jnp.zeros((16 - LOCAL - UPPER, TOK), jnp.float32)], 0
    )
    keys, queries = b_ref[...], c_ref[...]
    inputs, grads = x_ref[...].astype(jnp.float32), g_ref[...].astype(jnp.float32)

    lend_ref[0:CHAN, :] = inputs
    lend_ref[CHAN : 2 * CHAN, :] = grads

    def put(place, value):
        for half in range(2):
            msg_ref[pl.ds(2 * place + half, SHARDS, stride=ROWS), :] = value[
                half * SHARDS : (half + 1) * SHARDS
            ]

    high, low = split2(inputs * leave)
    put(0, mm(high, keys) + mm(low, keys))
    for level in range(UPPER):
        high, low = split2(grads * (gates_ref[LOCAL + level : LOCAL + level + 1, :] * entry))
        put(1 + level, mm(high, queries) + mm(low, queries))
    msg_ref[pl.ds(GAIN_ROW, SHARDS, stride=ROWS), :] = jnp.broadcast_to(last, (SHARDS, STATE))
    for spare in range(GAIN_ROW + 1, ROWS):
        msg_ref[pl.ds(spare, SHARDS, stride=ROWS), :] = jnp.zeros((SHARDS, STATE), jnp.float32)


def chain_kernel(in_ref, lent_ref, out_ref):
    del lent_ref

    def send(row, value):
        for member in range(PAIR):
            out_ref[pl.ds(member * ROWS + row, SHARDS, stride=PAIR * ROWS), :] = value

    def get(row):
        return in_ref[pl.ds(row, SHARDS, stride=ROWS), :]

    def pair(place):
        return jnp.concatenate([get(2 * place), get(2 * place + 1)], 1)

    logs = get(GAIN_ROW)
    near = logs[:, :SHARDS]
    here, there = iota((SHARDS, SHARDS), 0), iota((SHARDS, SHARDS), 1)
    before = (there < here).astype(jnp.float32).astype(jnp.bfloat16)
    after = (there > here).astype(jnp.float32).astype(jnp.bfloat16)
    gain_before = jnp.exp(sum(mm(before, part) for part in split3(jnp.where(here > there, near, 0.0))))
    gain_after = jnp.exp(sum(mm(after, part) for part in split3(jnp.where(here < there, near, 0.0))))
    lanes = iota((SHARDS, 2 * STATE), 0)
    end_state = pair(0)
    picks = []
    for level in range(UPPER):
        block = (here >> (level + 1)) == (there >> (level + 1))
        early = ((there >> level) & 1) == 0
        picks.append(jnp.where(block & early & (there < here), gain_before, 0.0))
    prefix = mm_split(jnp.concatenate(picks, 0), end_state)
    returned = jnp.zeros((SHARDS, 2 * STATE), jnp.float32)
    gain_grad = jnp.zeros((SHARDS, 2 * STATE), jnp.float32)

    def put(place, value):
        for half in range(2):
            send(2 * place + half, value[:, half * STATE : (half + 1) * STATE])

    for level in range(UPPER):
        block = (here >> (level + 1)) == (there >> (level + 1))
        late = ((there >> level) & 1) == 1
        pick = jnp.where(block & late & (there > here), gain_after, 0.0)
        suffix = mm_split(pick, pair(1 + level))
        front = prefix[level * SHARDS : (level + 1) * SHARDS]
        upper = ((lanes >> level) & 1) == 1
        put(1 + level, jnp.where(upper, front, 0.0))
        returned = returned + jnp.where(upper, 0.0, suffix)
        gain_grad = gain_grad + front * suffix
    put(0, returned)
    gain = (gain_grad[:, :STATE] + gain_grad[:, STATE:]) * jnp.exp(logs)
    send(GAIN_ROW, gain)
    for spare in range(GAIN_ROW + 1, ROWS):
        send(spare, jnp.zeros((SHARDS, STATE), jnp.float32))


def within_kernel(
    x_ref,
    g_ref,
    b_ref,
    c_ref,
    gates_ref,
    rows_ref,
    vals_ref,
    totals_ref,
    sums_ref,
    flow_ref,
    keys_ref,
    queries_ref,
):
    columns = jnp.transpose(rows_ref[...])
    run_col, count_col = columns[:, 0:1], columns[:, 1:2]
    x_t = jnp.transpose(x_ref[...].astype(jnp.float32)).astype(jnp.bfloat16)
    keys_t = jnp.transpose(b_ref[...].astype(jnp.float32)).astype(jnp.bfloat16)
    lane = iota((1, BLOCK), 1)
    causal = iota((BLOCK, BLOCK), 0) <= iota((BLOCK, BLOCK), 1)
    blocks = TOK // BLOCK
    for late in range(blocks):
        first, stop = late * BLOCK, (late + 1) * BLOCK
        queries, grads = c_ref[first:stop, :], g_ref[:, first:stop]
        run_row, count_row = rows_ref[0:1, first:stop], rows_ref[1:2, first:stop]
        gate_rows = [gates_ref[level : level + 1, first:stop] for level in range(LOCAL)]
        level_sums = [jnp.zeros((1, BLOCK), jnp.float32) for _ in range(LOCAL)]
        scores_all = mm(b_ref[:stop, :], queries, NT)
        kernel_grad_all = mm(x_t[:stop], grads)
        kernel_parts, grad_parts = [], []
        for early in range(late + 1):
            low, high = early * BLOCK, (early + 1) * BLOCK
            scores, kernel_grad = scores_all[low:high], kernel_grad_all[low:high]
            valid = count_row == count_col[low:high]
            if early == late:
                valid = valid & causal
            decay = jnp.where(valid, jnp.exp(jnp.minimum(run_row - run_col[low:high], 0.0)), 0.0)
            if early == late:
                top = jnp.where(lane < SPAN, gate_rows[0], gate_rows[1])
                gate = jnp.concatenate(
                    [
                        jnp.broadcast_to(top, (SPAN, BLOCK)),
                        jnp.broadcast_to(gate_rows[0], (SPAN, BLOCK)),
                    ],
                    0,
                )
            else:
                level = 1 + (late ^ early).bit_length()
                gate = gate_rows[level]
            weight = gate * decay
            kernel_parts.append((scores * weight).astype(jnp.bfloat16))
            score_grad = kernel_grad * weight
            grad_parts.append(score_grad.astype(jnp.bfloat16))
            terms = kernel_grad * scores * decay
            if early == late:
                upper = jnp.sum(terms[:SPAN], axis=0, keepdims=True)
                lower = jnp.sum(terms[SPAN:], axis=0, keepdims=True)
                level_sums[0] = level_sums[0] + jnp.where(lane < SPAN, upper, 0.0) + lower
                level_sums[1] = level_sums[1] + jnp.where(lane < SPAN, 0.0, upper)
                flow_ref[low:high, :] = score_grad * scores
            else:
                level_sums[level] = level_sums[level] + jnp.sum(terms, axis=0, keepdims=True)
                flow_ref[low:high, :] = flow_ref[low:high, :] + score_grad * scores
        kernel_low = jnp.concatenate(kernel_parts, 0)
        score_grad = jnp.concatenate(grad_parts, 0)
        vals = mm(grads, kernel_low, NT)
        key_part = mm(score_grad, queries)
        queries_ref[:, first:stop] = mm(keys_t[:, :stop], score_grad)
        vals_ref[:, first:stop] = vals[:, first:stop]
        keys_ref[first:stop, :] = key_part[first:stop]
        if late:
            vals_ref[:, :first] = vals_ref[:, :first] + vals[:, :first]
            keys_ref[:first, :] = keys_ref[:first, :] + key_part[:first]
        sums_ref[0:LOCAL, first:stop] = jnp.concatenate(level_sums, 0)
    ones = jnp.ones((8, BLOCK), jnp.bfloat16)
    column_flow = sum(mm(ones, part, NT) for part in split3(flow_ref[...]))
    sums_ref[LOCAL : 2 * LOCAL, :] = column_flow[0:LOCAL]
    totals_ref[:, :STATE] = keys_ref[...]
    totals_ref[:, STATE:] = jnp.transpose(queries_ref[...])


def chunk_rows(chunk, side):
    return pl.ds(pl.multiple_of(chunk * PAIR * CHUNK + side * CHUNK, CHUNK), CHUNK)


def partner_kernel(
    side_ref,
    lent_ref,
    x_ref,
    g_ref,
    b_ref,
    c_ref,
    gates_ref,
    rows_ref,
    totals_ref,
    kept_ref,
    x_high_ref,
    x_low_ref,
    g_high_ref,
    g_low_ref,
    keys_ref,
    queries_ref,
    turned_queries_ref,
    x_ref_turned,
    g_ref_turned,
):
    side = side_ref[0]
    inputs, grads = lent_ref[0:CHAN, :], lent_ref[CHAN : 2 * CHAN, :]
    rows = lent_ref[LENT_ROWS:LENT_GATES, :]
    own_grads = g_ref[...].astype(jnp.float32)
    x_ref_turned[...] = jnp.transpose(
        jnp.concatenate([x_ref[...].astype(jnp.float32) * rows_ref[2:3, :], inputs * rows[2:3]], 0)
    )
    scaled = [
        own_grads * (gates_ref[level : level + 1, :] * rows_ref[3:4, :])
        for level in range(LOCAL, LOCAL + UPPER)
    ] + [
        grads * (lent_ref[LENT_GATES + level : LENT_GATES + level + 1, :] * rows[3:4])
        for level in range(LOCAL, LOCAL + UPPER)
    ]
    g_ref_turned[...] = jnp.transpose(jnp.concatenate(scaled, 0))

    columns = jnp.transpose(rows)
    run_col, count_col = columns[:, 0:1], columns[:, 1:2]
    x_t = jnp.transpose(inputs).astype(jnp.bfloat16)
    keys_t = jnp.transpose(b_ref[...].astype(jnp.float32)).astype(jnp.bfloat16)
    lane = iota((1, BLOCK), 1)
    causal = iota((BLOCK, BLOCK), 0) <= iota((BLOCK, BLOCK), 1)
    for late in range(TOK // BLOCK):
        first, stop = late * BLOCK, (late + 1) * BLOCK
        queries = c_ref[first:stop, :]
        run_row, count_row = rows[0:1, first:stop], rows[1:2, first:stop]
        gate_rows = [
            lent_ref[LENT_GATES + level : LENT_GATES + level + 1, first:stop] for level in range(LOCAL)
        ]
        kernel_grad_all = mm(x_t[:stop], grads[:, first:stop].astype(jnp.bfloat16))
        grad_parts = []
        for early in range(late + 1):
            low_row, high_row = early * BLOCK, (early + 1) * BLOCK
            valid = count_row == count_col[low_row:high_row]
            if early == late:
                valid = valid & causal
                top = jnp.where(lane < SPAN, gate_rows[0], gate_rows[1])
                gate = jnp.concatenate(
                    [
                        jnp.broadcast_to(top, (SPAN, BLOCK)),
                        jnp.broadcast_to(gate_rows[0], (SPAN, BLOCK)),
                    ],
                    0,
                )
            else:
                gate = gate_rows[1 + (late ^ early).bit_length()]
            spread = jnp.minimum(run_row - run_col[low_row:high_row], 0.0)
            decay = jnp.where(valid, jnp.exp(spread), 0.0)
            weight = gate * decay
            grad_parts.append((kernel_grad_all[low_row:high_row] * weight).astype(jnp.bfloat16))
        score_grad = jnp.concatenate(grad_parts, 0)
        key_part = mm(score_grad, queries)
        queries_ref[:, first:stop] = mm(keys_t[:, :stop], score_grad)
        keys_ref[first:stop, :] = key_part[first:stop]
        if late:
            keys_ref[:first, :] = keys_ref[:first, :] + key_part[:first]
    turned_queries_ref[...] = jnp.transpose(queries_ref[...])
    for chunk in range(HALF // CHUNK):
        place = slice(chunk * CHUNK, (chunk + 1) * CHUNK)
        here = chunk_rows(chunk, side)
        kept_ref[place, :STATE] = totals_ref[here, :STATE] + keys_ref[here, :]
        kept_ref[place, STATE:] = totals_ref[here, STATE:] + turned_queries_ref[here, :]
        turned_high, turned_low = split2(x_ref_turned[here, :])
        x_high_ref[place, :], x_low_ref[place, :] = turned_high, turned_low
        turned_high, turned_low = split2(g_ref_turned[here, :])
        g_high_ref[place, :], g_low_ref[place, :] = turned_high, turned_low


def cross_kernel(
    side_ref,
    msg_ref,
    x_ref,
    g_ref,
    b_ref,
    c_ref,
    gates_ref,
    rows_ref,
    vals_ref,
    sums_ref,
    kept_ref,
    x_high_ref,
    x_low_ref,
    g_high_ref,
    g_low_ref,
    grad_inputs_ref,
    totals_ref,
    grad_gates_ref,
    grad_decay_ref,
):
    first_side = side_ref[0] == 0

    def load(row, member):
        return msg_ref[pl.ds(member * ROWS + row, SHARDS, stride=PAIR * ROWS), :]

    def get(place):
        mine, other = [], []
        for half in range(2):
            even, odd = load(2 * place + half, 0), load(2 * place + half, 1)
            mine.append(jnp.where(first_side, even, odd))
            other.append(jnp.where(first_side, odd, even))
        return jnp.concatenate(mine, 0), jnp.concatenate(other, 0)

    leave, entry = rows_ref[2:3, :], rows_ref[3:4, :]
    inputs, grads = x_ref[...].astype(jnp.float32), g_ref[...].astype(jnp.float32)
    keys, queries = b_ref[...], c_ref[...]

    back_high, back_low = split2(jnp.concatenate(get(0), 0))
    pulled = (mm(back_high[:CHAN], keys, NT) + mm(back_low[:CHAN], keys, NT)) * leave
    grad_inputs_ref[...] = (vals_ref[...] + pulled).astype(jnp.bfloat16)
    pulled_flow = jnp.sum(inputs * pulled, axis=0, keepdims=True)
    totals_ref[:, :STATE] = (
        kept_ref[:, :STATE]
        + mm(x_high_ref[...], back_high)
        + mm(x_high_ref[...], back_low)
        + mm(x_low_ref[...], back_high)
    )

    states = [get(1 + level) for level in range(UPPER)]
    carried = [mine for mine, _ in states] + [other for _, other in states]
    front_high, front_low = split2(jnp.concatenate(carried, 0))
    totals_ref[:, STATE:] = (
        kept_ref[:, STATE:]
        + mm(g_high_ref[...], front_high)
        + mm(g_high_ref[...], front_low)
        + mm(g_low_ref[...], front_high)
    )
    own = UPPER * CHAN
    seen = mm(front_high[:own], queries, NT) + mm(front_low[:own], queries, NT)
    run_grad = -sums_ref[LOCAL : LOCAL + 1, :] - pulled_flow
    for level in range(LOCAL):
        gate_sum = sums_ref[level : level + 1, :]
        grad_gates_ref[level : level + 1, :] = gate_sum
        run_grad = run_grad + gates_ref[level : level + 1, :] * gate_sum
    for level in range(UPPER):
        row = slice(LOCAL + level, LOCAL + level + 1)
        gate = gates_ref[row, :]
        cross_value = jnp.sum(
            grads * seen[level * CHAN : (level + 1) * CHAN], axis=0, keepdims=True
        )
        grad_gate = entry * cross_value
        grad_gates_ref[row, :] = grad_gate
        run_grad = run_grad + gate * grad_gate

    gain = jnp.where(first_side, load(GAIN_ROW, 0), load(GAIN_ROW, 1))
    gain = jnp.sum(gain, axis=0, keepdims=True)
    gain = jnp.sum(gain, axis=1, keepdims=True) + jnp.sum(pulled_flow, axis=1, keepdims=True)
    run_grad = run_grad + jnp.where(iota((1, TOK), 1) == TOK - 1, gain, 0.0)
    grad_decay_ref[...] = row_sums(run_grad, backward=True)


def f32(*shape):
    return jax.ShapeDtypeStruct(shape, jnp.float32)


def near(*shape, dtype=jnp.float32):
    return pltpu.VMEM(shape, dtype)


def hold(value):
    return pltpu.with_memory_space_constraint(value, pltpu.VMEM)


def low(*shape):
    return jax.ShapeDtypeStruct(shape, jnp.bfloat16)


def cost(flops, moved):
    return pl.CostEstimate(flops=flops, bytes_accessed=moved, transcendentals=0)


def local_states(inputs, grad_out, keys_b, queries_c, level_gates, log_decay, doc_starts):
    vmem = pl.BlockSpec(memory_space=pltpu.VMEM)
    return pl.pallas_call(
        states_kernel,
        out_shape=(near(SHARDS * ROWS, STATE), near(8, TOK), near(LEND, TOK)),
        in_specs=[vmem] * 6 + [pl.BlockSpec(memory_space=pltpu.SMEM)],
        out_specs=(vmem, vmem, vmem),
        cost_estimate=cost(100_000_000, 700_000),
        name="states",
    )(inputs, grad_out, keys_b, queries_c, level_gates, log_decay, doc_starts)


def chains(messages, lent):
    return pl.pallas_call(
        chain_kernel,
        out_shape=near(PAIR * SHARDS * ROWS, STATE),
        in_specs=[pl.BlockSpec(memory_space=pltpu.VMEM)] * 2,
        out_specs=pl.BlockSpec(memory_space=pltpu.VMEM),
        cost_estimate=cost(20_000_000, 500_000),
        name="chains",
    )(hold(messages), hold(lent))


def within_terms(inputs, grad_out, keys_b, queries_c, level_gates, rows):
    vmem = pl.BlockSpec(memory_space=pltpu.VMEM)
    return pl.pallas_call(
        within_kernel,
        out_shape=(
            near(CHAN, TOK),
            near(TOK, 2 * STATE),
            near(2 * LOCAL, TOK),
        ),
        in_specs=[vmem] * 6,
        out_specs=(vmem,) * 3,
        scratch_shapes=[
            pltpu.VMEM((TOK, BLOCK), jnp.float32),
            pltpu.VMEM((TOK, STATE), jnp.float32),
            pltpu.VMEM((STATE, TOK), jnp.float32),
        ],
        cost_estimate=cost(4_000_000_000, 1_000_000),
        name="within",
    )(*[hold(part) for part in (inputs, grad_out, keys_b, queries_c, level_gates, rows)])


def partner_terms(side, lent, inputs, grad_out, keys_b, queries_c, level_gates, rows, totals):
    vmem = pl.BlockSpec(memory_space=pltpu.VMEM)
    return pl.pallas_call(
        partner_kernel,
        out_shape=(
            near(HALF, 2 * STATE),
            near(HALF, PAIR * CHAN, dtype=jnp.bfloat16),
            near(HALF, PAIR * CHAN, dtype=jnp.bfloat16),
            near(HALF, PAIR * UPPER * CHAN, dtype=jnp.bfloat16),
            near(HALF, PAIR * UPPER * CHAN, dtype=jnp.bfloat16),
        ),
        in_specs=[pl.BlockSpec(memory_space=pltpu.SMEM)] + [vmem] * 8,
        out_specs=(vmem,) * 5,
        scratch_shapes=[
            pltpu.VMEM((TOK, STATE), jnp.float32),
            pltpu.VMEM((STATE, TOK), jnp.float32),
            pltpu.VMEM((TOK, STATE), jnp.float32),
            pltpu.VMEM((TOK, PAIR * CHAN), jnp.float32),
            pltpu.VMEM((TOK, PAIR * UPPER * CHAN), jnp.float32),
        ],
        cost_estimate=cost(4_000_000_000, 2_000_000),
        name="partner",
    )(
        side,
        *[
            hold(part)
            for part in (lent, inputs, grad_out, keys_b, queries_c, level_gates, rows, totals)
        ],
    )


def cross_terms(side, messages, inputs, grad_out, keys_b, queries_c, level_gates, rows, within):
    vmem = pl.BlockSpec(memory_space=pltpu.VMEM)
    return pl.pallas_call(
        cross_kernel,
        out_shape=(
            low(CHAN, TOK),
            near(HALF, 2 * STATE),
            f32(LOCAL + UPPER, TOK),
            f32(1, TOK),
        ),
        in_specs=[pl.BlockSpec(memory_space=pltpu.SMEM)] + [vmem] * 14,
        out_specs=(vmem,) * 4,
        cost_estimate=cost(300_000_000, 2_000_000),
        name="cross",
    )(
        side,
        *[
            hold(part)
            for part in (messages, inputs, grad_out, keys_b, queries_c, level_gates, rows, *within)
        ]
    )


def shards(inputs, grad_out, keys_b, queries_c, level_gates, log_decay, doc_starts):
    heads = lax.axis_size("head")
    side = (lax.axis_index("head") % PAIR).astype(jnp.int32).reshape(1)
    messages, rows, lend = local_states(
        inputs, grad_out, keys_b, queries_c, level_gates, log_decay, doc_starts
    )
    arrived = lax.all_to_all(messages.reshape(SHARDS, ROWS, STATE), "seq", 0, 0, tiled=True)
    lent = lax.ppermute(lend, "head", [(head, head ^ 1) for head in range(heads)])
    given = (inputs, grad_out, keys_b, queries_c, level_gates, rows)
    vals, totals, sums = within_terms(*given)
    answers = chains(arrived.reshape(SHARDS * ROWS, STATE), lent)
    pairs = [
        [shard * heads + head + member for shard in range(SHARDS) for member in range(PAIR)]
        for head in range(0, heads, PAIR)
    ]
    answers = lax.all_to_all(
        answers.reshape(PAIR * SHARDS, ROWS, STATE),
        ("seq", "head"),
        0,
        0,
        axis_index_groups=pairs,
        tiled=True,
    ).reshape(PAIR * SHARDS * ROWS, STATE)
    both = partner_terms(side, lent, *given, totals)
    grad_inputs, totals, grad_gates, grad_decay = cross_terms(
        side, answers, *given, (vals, sums, *both)
    )
    sides = [list(range(start, heads, PAIR)) for start in range(PAIR)]
    parts = lax.all_to_all(
        totals.reshape(heads // PAIR, CHUNK, 2 * STATE),
        "head",
        0,
        0,
        axis_index_groups=sides,
        tiled=True,
    )
    total = jnp.sum(parts, axis=0).astype(jnp.bfloat16)
    return grad_inputs, total[:, :STATE], total[:, STATE:], grad_gates, grad_decay


def solution(mesh):
    by_head = P("head", "seq")
    in_specs = (by_head, by_head, P("seq", None), P("seq", None), by_head, by_head, P("seq"))
    out_specs = (by_head, P(("seq", "head"), None), P(("seq", "head"), None), by_head, by_head)
    return jax.shard_map(shards, mesh=mesh, in_specs=in_specs, out_specs=out_specs, check_vma=False)
```

```python
import jax
import jax.numpy as jnp
from jax import lax
from jax.experimental import pallas as pl
from jax.experimental.pallas import tpu as pltpu
from jax.sharding import PartitionSpec as P

SPAN = 64
SPANS = 8
TOK = 512
CHAN = 64
STATE = 128
LOCAL = 4
UPPER = 5
SHARDS = 32
ROWS = 16
GAIN_ROW = 2 * (UPPER + 1)
BLOCK = 128
PAIR = 2
CHUNK = 32
HALF = TOK // PAIR
LENT_ROWS = 2 * CHAN
LENT_GATES = LENT_ROWS + 8
LEND = LENT_GATES + 16

NN = (((1,), (0,)), ((), ()))
NT = (((1,), (1,)), ((), ()))


def mm(left, right, dims=NN, precision=None):
    return lax.dot_general(
        left, right, dims, precision=precision, preferred_element_type=jnp.float32
    )


def split2(value):
    high = value.astype(jnp.bfloat16)
    return high, (value - high.astype(jnp.float32)).astype(jnp.bfloat16)


def mm_split(left, right):
    left_high, left_low = split2(left)
    right_high, right_low = split2(right)
    return mm(left_high, right_high) + mm(left_high, right_low) + mm(left_low, right_high)


def split3(value):
    high, rest = split2(value)
    rest = value - high.astype(jnp.float32)
    return (high,) + split2(rest)


def iota(shape, axis):
    return lax.broadcasted_iota(jnp.int32, shape, axis)


def row_sums(row, backward=False):
    blocks = TOK // BLOCK
    stack = jnp.concatenate([row[:, at * BLOCK : (at + 1) * BLOCK] for at in range(blocks)], 0)
    parts = [part.astype(jnp.float32) for part in split3(stack)]
    parts.append(jnp.zeros((16 - 3 * blocks, BLOCK), jnp.float32))
    here, there = iota((BLOCK, BLOCK), 0), iota((BLOCK, BLOCK), 1)
    keep = (here >= there if backward else here <= there).astype(jnp.float32)
    out = mm(jnp.concatenate(parts, 0).astype(jnp.bfloat16), keep.astype(jnp.bfloat16))
    sums = out[0:blocks] + out[blocks : 2 * blocks] + out[2 * blocks : 3 * blocks]
    offset = jnp.zeros((1, 1), jnp.float32)
    pieces = []
    for at in range(blocks - 1, -1, -1) if backward else range(blocks):
        piece = sums[at : at + 1] + offset
        offset = piece[:, :1] if backward else piece[:, BLOCK - 1 :]
        pieces.append(piece)
    return jnp.concatenate(pieces[::-1] if backward else pieces, 1)


def states_kernel(x_ref, g_ref, b_ref, c_ref, gates_ref, decay_ref, starts_ref, msg_ref, rows_ref, lend_ref):
    run = row_sums(decay_ref[...])
    last = run[:, TOK - 1 : TOK]
    token = iota((1, TOK), 1)
    counts = jnp.zeros((1, TOK), jnp.int32)
    total = jnp.int32(0)
    for span in range(SPANS):
        counts = counts + jnp.where(token >= span * SPAN, starts_ref[span], 0)
        total = total + starts_ref[span]
    entry = jnp.where(counts == 0, jnp.exp(run), 0.0)
    leave = jnp.where(counts == total, jnp.exp(last - run), 0.0)
    rows = jnp.concatenate(
        [run, counts.astype(jnp.float32), leave, entry, jnp.zeros((4, TOK), jnp.float32)], 0
    )
    rows_ref[...] = rows
    lend_ref[LENT_ROWS:LENT_GATES, :] = rows
    lend_ref[LENT_GATES:, :] = jnp.concatenate(
        [gates_ref[...], jnp.zeros((16 - LOCAL - UPPER, TOK), jnp.float32)], 0
    )
    keys, queries = b_ref[...], c_ref[...]
    inputs, grads = x_ref[...].astype(jnp.float32), g_ref[...].astype(jnp.float32)

    lend_ref[0:CHAN, :] = inputs
    lend_ref[CHAN : 2 * CHAN, :] = grads

    def put(place, value):
        for half in range(2):
            msg_ref[pl.ds(2 * place + half, SHARDS, stride=ROWS), :] = value[
                half * SHARDS : (half + 1) * SHARDS
            ]

    high, low = split2(inputs * leave)
    put(0, mm(high, keys) + mm(low, keys))
    for level in range(UPPER):
        high, low = split2(grads * (gates_ref[LOCAL + level : LOCAL + level + 1, :] * entry))
        put(1 + level, mm(high, queries) + mm(low, queries))
    msg_ref[pl.ds(GAIN_ROW, SHARDS, stride=ROWS), :] = jnp.broadcast_to(last, (SHARDS, STATE))
    for spare in range(GAIN_ROW + 1, ROWS):
        msg_ref[pl.ds(spare, SHARDS, stride=ROWS), :] = jnp.zeros((SHARDS, STATE), jnp.float32)


def chain_kernel(in_ref, lent_ref, sums_ref, out_ref):
    del lent_ref, sums_ref

    def send(row, value):
        for member in range(PAIR):
            out_ref[pl.ds(member * ROWS + row, SHARDS, stride=PAIR * ROWS), :] = value

    def get(row):
        return in_ref[pl.ds(row, SHARDS, stride=ROWS), :]

    def pair(place):
        return jnp.concatenate([get(2 * place), get(2 * place + 1)], 1)

    logs = get(GAIN_ROW)
    near = logs[:, :SHARDS]
    here, there = iota((SHARDS, SHARDS), 0), iota((SHARDS, SHARDS), 1)
    before = (there < here).astype(jnp.float32).astype(jnp.bfloat16)
    after = (there > here).astype(jnp.float32).astype(jnp.bfloat16)
    gain_before = jnp.exp(sum(mm(before, part) for part in split3(jnp.where(here > there, near, 0.0))))
    gain_after = jnp.exp(sum(mm(after, part) for part in split3(jnp.where(here < there, near, 0.0))))
    lanes = iota((SHARDS, 2 * STATE), 0)
    end_state = pair(0)
    picks = []
    for level in range(UPPER):
        block = (here >> (level + 1)) == (there >> (level + 1))
        early = ((there >> level) & 1) == 0
        picks.append(jnp.where(block & early & (there < here), gain_before, 0.0))
    prefix = mm_split(jnp.concatenate(picks, 0), end_state)
    returned = jnp.zeros((SHARDS, 2 * STATE), jnp.float32)
    gain_grad = jnp.zeros((SHARDS, 2 * STATE), jnp.float32)

    def put(place, value):
        for half in range(2):
            send(2 * place + half, value[:, half * STATE : (half + 1) * STATE])

    for level in range(UPPER):
        block = (here >> (level + 1)) == (there >> (level + 1))
        late = ((there >> level) & 1) == 1
        pick = jnp.where(block & late & (there > here), gain_after, 0.0)
        suffix = mm_split(pick, pair(1 + level))
        front = prefix[level * SHARDS : (level + 1) * SHARDS]
        upper = ((lanes >> level) & 1) == 1
        put(1 + level, jnp.where(upper, front, 0.0))
        returned = returned + jnp.where(upper, 0.0, suffix)
        gain_grad = gain_grad + front * suffix
    put(0, returned)
    gain = (gain_grad[:, :STATE] + gain_grad[:, STATE:]) * jnp.exp(logs)
    send(GAIN_ROW, gain)
    for spare in range(GAIN_ROW + 1, ROWS):
        send(spare, jnp.zeros((SHARDS, STATE), jnp.float32))


def within_kernel(
    x_ref,
    g_ref,
    b_ref,
    c_ref,
    gates_ref,
    rows_ref,
    vals_ref,
    totals_ref,
    sums_ref,
    flow_ref,
    keys_ref,
    queries_ref,
):
    columns = jnp.transpose(rows_ref[...])
    run_col, count_col = columns[:, 0:1], columns[:, 1:2]
    x_t = jnp.transpose(x_ref[...].astype(jnp.float32)).astype(jnp.bfloat16)
    keys_t = jnp.transpose(b_ref[...].astype(jnp.float32)).astype(jnp.bfloat16)
    lane = iota((1, BLOCK), 1)
    causal = iota((BLOCK, BLOCK), 0) <= iota((BLOCK, BLOCK), 1)
    blocks = TOK // BLOCK
    for late in range(blocks):
        first, stop = late * BLOCK, (late + 1) * BLOCK
        queries, grads = c_ref[first:stop, :], g_ref[:, first:stop]
        run_row, count_row = rows_ref[0:1, first:stop], rows_ref[1:2, first:stop]
        gate_rows = [gates_ref[level : level + 1, first:stop] for level in range(LOCAL)]
        level_sums = [jnp.zeros((1, BLOCK), jnp.float32) for _ in range(LOCAL)]
        scores_all = mm(b_ref[:stop, :], queries, NT)
        kernel_grad_all = mm(x_t[:stop], grads)
        kernel_parts, grad_parts = [], []
        for early in range(late + 1):
            low, high = early * BLOCK, (early + 1) * BLOCK
            scores, kernel_grad = scores_all[low:high], kernel_grad_all[low:high]
            valid = count_row == count_col[low:high]
            if early == late:
                valid = valid & causal
            decay = jnp.where(valid, jnp.exp(jnp.minimum(run_row - run_col[low:high], 0.0)), 0.0)
            if early == late:
                top = jnp.where(lane < SPAN, gate_rows[0], gate_rows[1])
                gate = jnp.concatenate(
                    [
                        jnp.broadcast_to(top, (SPAN, BLOCK)),
                        jnp.broadcast_to(gate_rows[0], (SPAN, BLOCK)),
                    ],
                    0,
                )
            else:
                level = 1 + (late ^ early).bit_length()
                gate = gate_rows[level]
            weight = gate * decay
            kernel_parts.append((scores * weight).astype(jnp.bfloat16))
            score_grad = kernel_grad * weight
            grad_parts.append(score_grad.astype(jnp.bfloat16))
            terms = kernel_grad * scores * decay
            if early == late:
                upper = jnp.sum(terms[:SPAN], axis=0, keepdims=True)
                lower = jnp.sum(terms[SPAN:], axis=0, keepdims=True)
                level_sums[0] = level_sums[0] + jnp.where(lane < SPAN, upper, 0.0) + lower
                level_sums[1] = level_sums[1] + jnp.where(lane < SPAN, 0.0, upper)
                flow_ref[low:high, :] = score_grad * scores
            else:
                level_sums[level] = level_sums[level] + jnp.sum(terms, axis=0, keepdims=True)
                flow_ref[low:high, :] = flow_ref[low:high, :] + score_grad * scores
        kernel_low = jnp.concatenate(kernel_parts, 0)
        score_grad = jnp.concatenate(grad_parts, 0)
        vals = mm(grads, kernel_low, NT)
        key_part = mm(score_grad, queries)
        queries_ref[:, first:stop] = mm(keys_t[:, :stop], score_grad)
        vals_ref[:, first:stop] = vals[:, first:stop]
        keys_ref[first:stop, :] = key_part[first:stop]
        if late:
            vals_ref[:, :first] = vals_ref[:, :first] + vals[:, :first]
            keys_ref[:first, :] = keys_ref[:first, :] + key_part[:first]
        sums_ref[0:LOCAL, first:stop] = jnp.concatenate(level_sums, 0)
    ones = jnp.ones((8, BLOCK), jnp.bfloat16)
    column_flow = sum(mm(ones, part, NT) for part in split3(flow_ref[...]))
    sums_ref[LOCAL : 2 * LOCAL, :] = column_flow[0:LOCAL]
    totals_ref[:, :STATE] = keys_ref[...]
    totals_ref[:, STATE:] = jnp.transpose(queries_ref[...])


def chunk_rows(chunk, side):
    return pl.ds(pl.multiple_of(chunk * PAIR * CHUNK + side * CHUNK, CHUNK), CHUNK)


def partner_kernel(
    side_ref,
    lent_ref,
    x_ref,
    g_ref,
    b_ref,
    c_ref,
    gates_ref,
    rows_ref,
    totals_ref,
    kept_ref,
    x_high_ref,
    x_low_ref,
    g_high_ref,
    g_low_ref,
    keys_ref,
    queries_ref,
    turned_queries_ref,
    x_ref_turned,
    g_ref_turned,
):
    side = side_ref[0]
    inputs, grads = lent_ref[0:CHAN, :], lent_ref[CHAN : 2 * CHAN, :]
    rows = lent_ref[LENT_ROWS:LENT_GATES, :]
    own_grads = g_ref[...].astype(jnp.float32)
    x_ref_turned[...] = jnp.transpose(
        jnp.concatenate([x_ref[...].astype(jnp.float32) * rows_ref[2:3, :], inputs * rows[2:3]], 0)
    )
    scaled = [
        own_grads * (gates_ref[level : level + 1, :] * rows_ref[3:4, :])
        for level in range(LOCAL, LOCAL + UPPER)
    ] + [
        grads * (lent_ref[LENT_GATES + level : LENT_GATES + level + 1, :] * rows[3:4])
        for level in range(LOCAL, LOCAL + UPPER)
    ]
    g_ref_turned[...] = jnp.transpose(jnp.concatenate(scaled, 0))

    columns = jnp.transpose(rows)
    run_col, count_col = columns[:, 0:1], columns[:, 1:2]
    x_t = jnp.transpose(inputs).astype(jnp.bfloat16)
    keys_t = jnp.transpose(b_ref[...].astype(jnp.float32)).astype(jnp.bfloat16)
    lane = iota((1, BLOCK), 1)
    causal = iota((BLOCK, BLOCK), 0) <= iota((BLOCK, BLOCK), 1)
    for late in range(TOK // BLOCK):
        first, stop = late * BLOCK, (late + 1) * BLOCK
        queries = c_ref[first:stop, :]
        run_row, count_row = rows[0:1, first:stop], rows[1:2, first:stop]
        gate_rows = [
            lent_ref[LENT_GATES + level : LENT_GATES + level + 1, first:stop] for level in range(LOCAL)
        ]
        kernel_grad_all = mm(x_t[:stop], grads[:, first:stop].astype(jnp.bfloat16))
        grad_parts = []
        for early in range(late + 1):
            low_row, high_row = early * BLOCK, (early + 1) * BLOCK
            valid = count_row == count_col[low_row:high_row]
            if early == late:
                valid = valid & causal
                top = jnp.where(lane < SPAN, gate_rows[0], gate_rows[1])
                gate = jnp.concatenate(
                    [
                        jnp.broadcast_to(top, (SPAN, BLOCK)),
                        jnp.broadcast_to(gate_rows[0], (SPAN, BLOCK)),
                    ],
                    0,
                )
            else:
                gate = gate_rows[1 + (late ^ early).bit_length()]
            spread = jnp.minimum(run_row - run_col[low_row:high_row], 0.0)
            decay = jnp.where(valid, jnp.exp(spread), 0.0)
            weight = gate * decay
            grad_parts.append((kernel_grad_all[low_row:high_row] * weight).astype(jnp.bfloat16))
        score_grad = jnp.concatenate(grad_parts, 0)
        key_part = mm(score_grad, queries)
        queries_ref[:, first:stop] = mm(keys_t[:, :stop], score_grad)
        keys_ref[first:stop, :] = key_part[first:stop]
        if late:
            keys_ref[:first, :] = keys_ref[:first, :] + key_part[:first]
    turned_queries_ref[...] = jnp.transpose(queries_ref[...])
    for chunk in range(HALF // CHUNK):
        place = slice(chunk * CHUNK, (chunk + 1) * CHUNK)
        here = chunk_rows(chunk, side)
        kept_ref[place, :STATE] = totals_ref[here, :STATE] + keys_ref[here, :]
        kept_ref[place, STATE:] = totals_ref[here, STATE:] + turned_queries_ref[here, :]
        turned_high, turned_low = split2(x_ref_turned[here, :])
        x_high_ref[place, :], x_low_ref[place, :] = turned_high, turned_low
        turned_high, turned_low = split2(g_ref_turned[here, :])
        g_high_ref[place, :], g_low_ref[place, :] = turned_high, turned_low


def cross_kernel(
    side_ref,
    msg_ref,
    x_ref,
    g_ref,
    b_ref,
    c_ref,
    gates_ref,
    rows_ref,
    vals_ref,
    sums_ref,
    kept_ref,
    x_high_ref,
    x_low_ref,
    g_high_ref,
    g_low_ref,
    grad_inputs_ref,
    totals_ref,
    grad_gates_ref,
    grad_decay_ref,
):
    first_side = side_ref[0] == 0

    def load(row, member):
        return msg_ref[pl.ds(member * ROWS + row, SHARDS, stride=PAIR * ROWS), :]

    def get(place):
        mine, other = [], []
        for half in range(2):
            even, odd = load(2 * place + half, 0), load(2 * place + half, 1)
            mine.append(jnp.where(first_side, even, odd))
            other.append(jnp.where(first_side, odd, even))
        return jnp.concatenate(mine, 0), jnp.concatenate(other, 0)

    leave, entry = rows_ref[2:3, :], rows_ref[3:4, :]
    inputs, grads = x_ref[...].astype(jnp.float32), g_ref[...].astype(jnp.float32)
    keys, queries = b_ref[...], c_ref[...]

    back_high, back_low = split2(jnp.concatenate(get(0), 0))
    pulled = (mm(back_high[:CHAN], keys, NT) + mm(back_low[:CHAN], keys, NT)) * leave
    grad_inputs_ref[...] = (vals_ref[...] + pulled).astype(jnp.bfloat16)
    pulled_flow = jnp.sum(inputs * pulled, axis=0, keepdims=True)
    totals_ref[:, :STATE] = (
        kept_ref[:, :STATE]
        + mm(x_high_ref[...], back_high)
        + mm(x_high_ref[...], back_low)
        + mm(x_low_ref[...], back_high)
    )

    states = [get(1 + level) for level in range(UPPER)]
    carried = [mine for mine, _ in states] + [other for _, other in states]
    front_high, front_low = split2(jnp.concatenate(carried, 0))
    totals_ref[:, STATE:] = (
        kept_ref[:, STATE:]
        + mm(g_high_ref[...], front_high)
        + mm(g_high_ref[...], front_low)
        + mm(g_low_ref[...], front_high)
    )
    own = UPPER * CHAN
    seen = mm(front_high[:own], queries, NT) + mm(front_low[:own], queries, NT)
    run_grad = -sums_ref[LOCAL : LOCAL + 1, :] - pulled_flow
    for level in range(LOCAL):
        gate_sum = sums_ref[level : level + 1, :]
        grad_gates_ref[level : level + 1, :] = gate_sum
        run_grad = run_grad + gates_ref[level : level + 1, :] * gate_sum
    for level in range(UPPER):
        row = slice(LOCAL + level, LOCAL + level + 1)
        gate = gates_ref[row, :]
        cross_value = jnp.sum(
            grads * seen[level * CHAN : (level + 1) * CHAN], axis=0, keepdims=True
        )
        grad_gate = entry * cross_value
        grad_gates_ref[row, :] = grad_gate
        run_grad = run_grad + gate * grad_gate

    gain = jnp.where(first_side, load(GAIN_ROW, 0), load(GAIN_ROW, 1))
    gain = jnp.sum(gain, axis=0, keepdims=True)
    gain = jnp.sum(gain, axis=1, keepdims=True) + jnp.sum(pulled_flow, axis=1, keepdims=True)
    run_grad = run_grad + jnp.where(iota((1, TOK), 1) == TOK - 1, gain, 0.0)
    grad_decay_ref[...] = row_sums(run_grad, backward=True)


def f32(*shape):
    return jax.ShapeDtypeStruct(shape, jnp.float32)


def near(*shape, dtype=jnp.float32):
    return pltpu.VMEM(shape, dtype)


def hold(value):
    return pltpu.with_memory_space_constraint(value, pltpu.VMEM)


def low(*shape):
    return jax.ShapeDtypeStruct(shape, jnp.bfloat16)


def cost(flops, moved):
    return pl.CostEstimate(flops=flops, bytes_accessed=moved, transcendentals=0)


def local_states(inputs, grad_out, keys_b, queries_c, level_gates, log_decay, doc_starts):
    vmem = pl.BlockSpec(memory_space=pltpu.VMEM)
    return pl.pallas_call(
        states_kernel,
        out_shape=(near(SHARDS * ROWS, STATE), near(8, TOK), near(LEND, TOK)),
        in_specs=[vmem] * 6 + [pl.BlockSpec(memory_space=pltpu.SMEM)],
        out_specs=(vmem, vmem, vmem),
        cost_estimate=cost(100_000_000, 700_000),
        name="states",
    )(inputs, grad_out, keys_b, queries_c, level_gates, log_decay, doc_starts)


def chains(messages, lent, sums):
    return pl.pallas_call(
        chain_kernel,
        out_shape=near(PAIR * SHARDS * ROWS, STATE),
        in_specs=[pl.BlockSpec(memory_space=pltpu.VMEM)] * 3,
        out_specs=pl.BlockSpec(memory_space=pltpu.VMEM),
        cost_estimate=cost(20_000_000, 500_000),
        name="chains",
    )(hold(messages), hold(lent), hold(sums))


def within_terms(inputs, grad_out, keys_b, queries_c, level_gates, rows):
    vmem = pl.BlockSpec(memory_space=pltpu.VMEM)
    return pl.pallas_call(
        within_kernel,
        out_shape=(
            near(CHAN, TOK),
            near(TOK, 2 * STATE),
            near(2 * LOCAL, TOK),
        ),
        in_specs=[vmem] * 6,
        out_specs=(vmem,) * 3,
        scratch_shapes=[
            pltpu.VMEM((TOK, BLOCK), jnp.float32),
            pltpu.VMEM((TOK, STATE), jnp.float32),
            pltpu.VMEM((STATE, TOK), jnp.float32),
        ],
        cost_estimate=cost(4_000_000_000, 1_000_000),
        name="within",
    )(*[hold(part) for part in (inputs, grad_out, keys_b, queries_c, level_gates, rows)])


def partner_terms(side, lent, inputs, grad_out, keys_b, queries_c, level_gates, rows, totals):
    vmem = pl.BlockSpec(memory_space=pltpu.VMEM)
    return pl.pallas_call(
        partner_kernel,
        out_shape=(
            near(HALF, 2 * STATE),
            near(HALF, PAIR * CHAN, dtype=jnp.bfloat16),
            near(HALF, PAIR * CHAN, dtype=jnp.bfloat16),
            near(HALF, PAIR * UPPER * CHAN, dtype=jnp.bfloat16),
            near(HALF, PAIR * UPPER * CHAN, dtype=jnp.bfloat16),
        ),
        in_specs=[pl.BlockSpec(memory_space=pltpu.SMEM)] + [vmem] * 8,
        out_specs=(vmem,) * 5,
        scratch_shapes=[
            pltpu.VMEM((TOK, STATE), jnp.float32),
            pltpu.VMEM((STATE, TOK), jnp.float32),
            pltpu.VMEM((TOK, STATE), jnp.float32),
            pltpu.VMEM((TOK, PAIR * CHAN), jnp.float32),
            pltpu.VMEM((TOK, PAIR * UPPER * CHAN), jnp.float32),
        ],
        cost_estimate=cost(4_000_000_000, 2_000_000),
        name="partner",
    )(
        side,
        *[
            hold(part)
            for part in (lent, inputs, grad_out, keys_b, queries_c, level_gates, rows, totals)
        ],
    )


def cross_terms(side, messages, inputs, grad_out, keys_b, queries_c, level_gates, rows, within):
    vmem = pl.BlockSpec(memory_space=pltpu.VMEM)
    return pl.pallas_call(
        cross_kernel,
        out_shape=(
            low(CHAN, TOK),
            near(HALF, 2 * STATE),
            f32(LOCAL + UPPER, TOK),
            f32(1, TOK),
        ),
        in_specs=[pl.BlockSpec(memory_space=pltpu.SMEM)] + [vmem] * 14,
        out_specs=(vmem,) * 4,
        cost_estimate=cost(300_000_000, 2_000_000),
        name="cross",
    )(
        side,
        *[
            hold(part)
            for part in (messages, inputs, grad_out, keys_b, queries_c, level_gates, rows, *within)
        ]
    )


def shards(inputs, grad_out, keys_b, queries_c, level_gates, log_decay, doc_starts):
    heads = lax.axis_size("head")
    side = (lax.axis_index("head") % PAIR).astype(jnp.int32).reshape(1)
    messages, rows, lend = local_states(
        inputs, grad_out, keys_b, queries_c, level_gates, log_decay, doc_starts
    )
    arrived = lax.all_to_all(messages.reshape(SHARDS, ROWS, STATE), "seq", 0, 0, tiled=True)
    lent = lax.ppermute(lend, "head", [(head, head ^ 1) for head in range(heads)])
    given = (inputs, grad_out, keys_b, queries_c, level_gates, rows)
    vals, totals, sums = within_terms(*given)
    answers = chains(arrived.reshape(SHARDS * ROWS, STATE), lent, sums)
    pairs = [
        [shard * heads + head + member for shard in range(SHARDS) for member in range(PAIR)]
        for head in range(0, heads, PAIR)
    ]
    answers = lax.all_to_all(
        answers.reshape(PAIR * SHARDS, ROWS, STATE),
        ("seq", "head"),
        0,
        0,
        axis_index_groups=pairs,
        tiled=True,
    ).reshape(PAIR * SHARDS * ROWS, STATE)
    both = partner_terms(side, lent, *given, totals)
    grad_inputs, totals, grad_gates, grad_decay = cross_terms(
        side, answers, *given, (vals, sums, *both)
    )
    sides = [list(range(start, heads, PAIR)) for start in range(PAIR)]
    parts = lax.all_to_all(
        totals.reshape(heads // PAIR, CHUNK, 2 * STATE),
        "head",
        0,
        0,
        axis_index_groups=sides,
        tiled=True,
    )
    total = jnp.sum(parts, axis=0).astype(jnp.bfloat16)
    return grad_inputs, total[:, :STATE], total[:, STATE:], grad_gates, grad_decay


def solution(mesh):
    by_head = P("head", "seq")
    in_specs = (by_head, by_head, P("seq", None), P("seq", None), by_head, by_head, P("seq"))
    out_specs = (by_head, P(("seq", "head"), None), P(("seq", "head"), None), by_head, by_head)
    return jax.shard_map(shards, mesh=mesh, in_specs=in_specs, out_specs=out_specs, check_vma=False)
```
